128 devices in a mesh: row: 4 (over z), col: 32 (over x, y, core).
Axes of the slice: x: 4, y: 4, z: 4, core: 2. Of those that a mesh axis runs over, the one named last changes fastest.
Arguments:
- image_features: float32 [16384, 1024], P(('row', 'col')), as said below
- text_features: float32 [16384, 1024], P(('col', 'row')), as said below
- logit_scale: float32 [1], replicated, may hold values from 4 to 4.6052
Outputs:
- mean_loss: float32 [1], replicated
- image_grad: float32 [16384, 1024], P(('row', 'col'))
- text_grad: float32 [16384, 1024], P(('col', 'row'))
- scale_grad: float32 [1], replicated
The draws below stay inside these ranges and needn't reach their ends.
Inputs may be any that keep to these rules, and one draw needn't show every extreme that they name: `image_features`: rows of the features have norms between about 1 and 16. `text_features`: rows of the features have norms between about 1 and 16.
All inputs are finite; a program needn't handle non-finite values.
Results may differ from the reference program's by a relative error of at most 0.0035.
Values may be sent and summed in bfloat16 or wider, within the bound.
A program may use at most 128 MiB of HBM per device.

```python
import math
import jax
import jax.numpy as jnp
from jax import lax

D = 1024
PAIRS = 16384


def assemble(noise, scale_key, log_spread):
    scales = jnp.exp(jax.random.uniform(scale_key, (PAIRS, 1), jnp.float32, 0.0, log_spread)) / 32.0
    picked = noise
    return picked * scales


def draw_image_features(key, part):
    key = jax.random.fold_in(key, 5)
    noise = jax.random.normal(key, (PAIRS, D), jnp.float32)
    return assemble(noise, jax.random.fold_in(key, 1), 2.3)


def draw_text_features(key, part):
    key = jax.random.fold_in(key, 7)
    noise = jax.random.normal(key, (PAIRS, D), jnp.float32)
    return assemble(noise, jax.random.fold_in(key, 1), 2.3)


def draw_logit_scale(key, part):
    key = jax.random.fold_in(key, 9)
    return jax.random.uniform(key, (1,), jnp.float32, 4.0, 4.4)


def setup_inputs(seed: int = 0) -> dict:
    arg_keys = jax.random.split(jax.random.key(seed), 4)
    return {
        "image_features": draw_image_features(jax.random.fold_in(arg_keys[3], 71), 0),
        "text_features": draw_text_features(jax.random.fold_in(arg_keys[3], 71), 0),
        "logit_scale": draw_logit_scale(jax.random.fold_in(arg_keys[3], 71), 0),
    }


EPS = 1e-06

def normalize(features):
    inverse = lax.rsqrt(lax.optimization_barrier(jnp.sum(features * features, axis=1, keepdims=True)) + EPS)
    return (features * inverse, inverse)

def contract_rows(left, right):
    return lax.dot_general(left, right, (((1,), (1,)), ((), ())), preferred_element_type=jnp.float32)

def reference(image_features, text_features, logit_scale):
    image_hat, image_inv = normalize(image_features)
    text_hat, text_inv = normalize(text_features)
    image_low = image_hat.astype(jnp.bfloat16)
    text_low = text_hat.astype(jnp.bfloat16)
    scale = jnp.exp(logit_scale[0])
    block = math.gcd(PAIRS, 512)
    steps = PAIRS // block
    image_blocks = image_low.reshape(steps, block, D)
    starts = jnp.arange(steps, dtype=jnp.int32) * block
    col_ids = lax.broadcasted_iota(jnp.int32, (1, PAIRS), 1)

    def forward(carry, item):
        col_peak, col_total = carry
        rows, start = item
        values = scale * contract_rows(rows, text_low)
        row_peak = lax.optimization_barrier(jnp.max(values, axis=1))
        row_lse = row_peak + jnp.log(lax.optimization_barrier(jnp.sum(jnp.exp(values - row_peak[:, None]), axis=1)))
        peak = jnp.maximum(col_peak, lax.optimization_barrier(jnp.max(values, axis=0)))
        col_total = col_total * jnp.exp(col_peak - peak) + lax.optimization_barrier(jnp.sum(jnp.exp(values - peak[None, :]), axis=0))
        return ((peak, col_total), row_lse)
    init = (jnp.full((PAIRS,), -jnp.inf, jnp.float32), jnp.zeros((PAIRS,), jnp.float32))
    (col_peak, col_total), row_lse = lax.scan(forward, init, (image_blocks, starts))
    col_lse = col_peak + jnp.log(col_total)
    row_lse = row_lse.reshape(PAIRS)
    diagonal = scale * lax.optimization_barrier(jnp.sum(image_low.astype(jnp.float32) * text_low.astype(jnp.float32), axis=1))
    mean_loss = (jnp.sum(row_lse) + jnp.sum(col_lse) - 2.0 * jnp.sum(diagonal)) / (2.0 * PAIRS)

    def backward(carry, item):
        text_sum, scale_sum = carry
        rows, start, lse_block = item
        values = scale * contract_rows(rows, text_low)
        row_ids = start + lax.broadcasted_iota(jnp.int32, (block, 1), 0)
        same = (row_ids == col_ids).astype(jnp.float32)
        probs = 0.5 * (jnp.exp(values - lse_block[:, None]) + jnp.exp(values - col_lse[None, :]))
        grad = probs - same
        grad_low = grad.astype(jnp.bfloat16)
        image_part = scale * jnp.dot(grad_low, text_low, preferred_element_type=jnp.float32)
        text_part = lax.dot_general(grad_low, rows, (((0,), (0,)), ((), ())), preferred_element_type=jnp.float32)
        return ((text_sum + scale * text_part, scale_sum + jnp.sum(grad * values)), image_part)
    init_back = (jnp.zeros((PAIRS, D), jnp.float32), jnp.zeros((), jnp.float32))
    (text_hat_grad, scale_sum), image_parts = lax.scan(backward, init_back, (image_blocks, starts, row_lse.reshape(steps, block)))
    image_hat_grad = image_parts.reshape(PAIRS, D)
    image_grad = image_inv * (image_hat_grad - image_hat * lax.optimization_barrier(jnp.sum(image_hat * image_hat_grad, axis=1, keepdims=True)))
    text_grad = text_inv * (text_hat_grad - text_hat * lax.optimization_barrier(jnp.sum(text_hat * text_hat_grad, axis=1, keepdims=True)))
    scale_grad = scale_sum / PAIRS
    return (mean_loss.reshape(1), image_grad, text_grad, scale_grad.reshape(1))
```

```python
import functools

import jax
import jax.numpy as jnp
from jax import lax
from jax.experimental import pallas as pl
from jax.experimental.pallas import tpu as pltpu
from jax.sharding import PartitionSpec as P

MESH = pl.DeviceIdType.MESH
EPS = 1e-06
LOG2E = 1.4426950408889634
LN2 = 0.6931471805599453
SHIFT = 34.0
TINY = 2.0**-60

CHUNK = 128
WIDTH = 1024
ORDER = (0, 1, 2, 4, 3, 5, 6, 7)
RANK = tuple(ORDER.index(q) for q in range(8))
PARTS = ((0, 48), (48, 48), (96, 32))
BF16 = jnp.bfloat16
F32 = jnp.float32


def stage_dim(part, stage):
    return (part + stage) % 3


def last_stage(q, part):
    stage = -1
    for t in range(3):
        if q >> stage_dim(part, t) & 1:
            stage = t
    return stage


def log2(x):
    return jnp.log(x) * LOG2E


def nt(a, b):
    return lax.dot_general(a, b, (((1,), (1,)), ((), ())), preferred_element_type=F32)


def nn(a, b):
    return lax.dot_general(a, b, (((1,), (0,)), ((), ())), preferred_element_type=F32)


def tn(a, b):
    return lax.dot_general(a, b, (((0,), (0,)), ((), ())), preferred_element_type=F32)


def flip_image(c):
    return c + 1 - 2 * lax.rem(c, 2)


def flip_text(c):
    return 3 - c


def kernel(
    scale_ref, image_ref, text_ref,
    image_out, text_out, sums_out,
    img, txt, u_s, grad_s, hi_s, lo_s, colhi_s, collo_s,
    rowl_s, rowl_r, coll_s, coll_r, rlse_s, clse_s, crow_s,
    a_img, a_txt, core_s, core_r, rs_s, rs_r,
    part_s, part_r, part2_s, part2_r,
    ag_send, ag_recv, core_send, core_recv,
    lse_send, lse_recv, csum_send, csum_recv, rs_send, rs_recv, tot_send, tot_recv,
):
    z = lax.axis_index("row")
    c = lax.axis_index("col")
    x, y, k = c // 8, lax.rem(c // 2, 4), lax.rem(c, 2)
    at = (x, y, z)
    flipped = (tuple(flip_image(v) for v in at), tuple(flip_text(v) for v in at))

    def place(side, q, other_core=0):
        px, py, pz = (flipped[side][d] if q >> d & 1 else at[d] for d in range(3))
        return {"row": pz, "col": (px * 4 + py) * 2 + (1 - k if other_core else k)}

    def remote(src, dst, send, recv, device):
        return pltpu.make_async_remote_copy(
            src_ref=src, dst_ref=dst, send_sem=send, recv_sem=recv, device_id=device, device_id_type=MESH
        )

    peers = [place(0, j >> 1, j & 1) for j in range(1, 16)] + [place(1, q) for q in range(1, 8)]
    barrier = pltpu.get_barrier_semaphore()
    for peer in peers:
        pl.semaphore_signal(barrier, inc=1, device_id=peer, device_id_type=MESH)

    def normalized(ref):
        v = ref[...]
        inverse = lax.rsqrt(jnp.sum(v * v, axis=1, keepdims=True) + EPS)
        return v * inverse, inverse

    img[pl.ds(0, CHUNK), :] = normalized(image_ref)[0].astype(BF16)
    txt[pl.ds(0, CHUNK), :] = normalized(text_ref)[0].astype(BF16)
    scale = jnp.exp(jnp.full((8, 128), scale_ref[0], F32))[0:1, 0:1]
    unit = scale * LOG2E
    hi_s[...] = jnp.zeros_like(hi_s)
    lo_s[...] = jnp.zeros_like(lo_s)
    colhi_s[...] = jnp.zeros_like(colhi_s)
    collo_s[...] = jnp.zeros_like(collo_s)

    pl.semaphore_wait(barrier, len(peers))

    def gather_rows(side, q, part):
        start, rows = PARTS[part]
        base = RANK[q] * (2 * CHUNK if side == 0 else CHUNK)
        return (img, txt)[side].at[pl.ds(base + start, rows)]

    def gather_copy(side, q, part):
        d = stage_dim(part, last_stage(q, part))
        i = (q - 1) * 3 + part
        return remote(
            gather_rows(side, q ^ (1 << d), part), gather_rows(side, q, part),
            ag_send.at[side, i], ag_recv.at[side, i], place(side, 1 << d),
        )

    def core_copy(q, part):
        start, rows = PARTS[part]
        base = RANK[q] * 2 * CHUNK + start
        return remote(
            img.at[pl.ds(base, rows)], img.at[pl.ds(base + CHUNK, rows)],
            core_send.at[q * 3 + part], core_recv.at[q * 3 + part], place(0, 0, 1),
        )

    def arrive(q, part, sides=(0, 1)):
        for side in sides:
            gather_copy(side, q, part).wait_recv()
            for t in range(last_stage(q, part) + 1, 3):
                gather_copy(side, q | 1 << stage_dim(part, t), part).start()
            if side == 0:
                core_copy(q, part).start()

    for t in range(3):
        for d in range(3):
            for side in range(2):
                gather_copy(side, 1 << d, (d - t) % 3).start()
    for part in range(3):
        core_copy(0, part).start()

    def scores(row0, rows, col0, cols):
        def block(i, _):
            r = pl.multiple_of(row0 + i * 256, 256)
            u = nt(img[pl.ds(r, 256), :], txt[pl.ds(col0, cols), :]) * unit
            u_s[pl.ds(r, 256), pl.ds(col0, cols)] = u
            hi = jnp.exp2(u - SHIFT)
            lo = jnp.exp2(jnp.minimum(u, 0.0) + SHIFT)
            for e, row_s, col_s in ((hi, hi_s, colhi_s), (lo, lo_s, collo_s)):
                row = e[:, 0:128]
                for j in range(1, cols // 128):
                    row = row + e[:, j * 128 : (j + 1) * 128]
                row_s[pl.ds(r, 256), :] += row
                col_s[:, pl.ds(col0, cols)] += jnp.sum(e.reshape(32, 8, cols), axis=0)
            return 0

        lax.fori_loop(0, rows // 256, block, 0)

    for part in range(3):
        arrive(1 << part, part)
    for d in range(3):
        arrive(1 << d, (d - 1) % 3)
    for d in range(3):
        arrive(1 << d, (d - 2) % 3)
    for q in (0, 1, 2, 4):
        for part in range(3):
            core_copy(q, part).wait_recv()
    scores(0, 1024, 0, 512)
    for d in range(3):
        arrive(1 << d | 1 << (d - 1) % 3, (d - 1) % 3)
    for d in range(3):
        arrive(1 << d | 1 << (d - 2) % 3, (d - 2) % 3)
    for d in range(3):
        arrive(1 << d | 1 << (d - 1) % 3, (d - 2) % 3)
    for q in (3, 5, 6):
        for part in range(3):
            core_copy(q, part).wait_recv()
    scores(0, 1792, 512, 256)
    scores(1024, 768, 0, 512)
    for d in range(3):
        arrive(7, (d - 2) % 3)
    for part in range(3):
        core_copy(7, part).wait_recv()
    scores(0, 2048, 768, 256)
    scores(1792, 256, 0, 768)

    def joined(hi, lo):
        return jnp.where(hi > TINY, log2(hi) + SHIFT, log2(lo) - SHIFT)

    def absolute(side, q):
        bits = [lax.rem(v, 2) for v in at] if side == 0 else [v // 2 for v in at]
        bits = [1 - b if q >> d & 1 else b for d, b in enumerate(bits)]
        return bits[0] + 2 * bits[1] + 4 * bits[2]

    def row_index(q, other):
        return absolute(0, q) * 2 + (1 - k if other else k)

    for q in range(8):
        for other in range(2):
            r = RANK[q] * 256 + other * CHUNK
            hi = jnp.sum(hi_s[pl.ds(r, CHUNK), :].T, axis=0, keepdims=True)
            lo = jnp.sum(lo_s[pl.ds(r, CHUNK), :].T, axis=0, keepdims=True)
            rowl_s[pl.ds(row_index(q, other), 1), :] = joined(hi, lo)
    colsum = joined(
        jnp.sum(colhi_s[...], axis=0, keepdims=True), jnp.sum(collo_s[...], axis=0, keepdims=True)
    )
    for q in range(8):
        coll_s[pl.ds(absolute(1, q), 1), :] = colsum[:, RANK[q] * 128 : (RANK[q] + 1) * 128]

    def row_copy(j):
        return remote(rowl_s, rowl_r.at[j - 1], lse_send.at[j - 1], lse_recv.at[j - 1], place(0, j >> 1, j & 1))

    def col_copy(q):
        return remote(coll_s, coll_r.at[q - 1], csum_send.at[q - 1], csum_recv.at[q - 1], place(1, q))

    for q in range(1, 8):
        col_copy(q).start()
    for j in range(1, 16):
        row_copy(j).start()
    for q in range(1, 8):
        col_copy(q).wait_recv()
    for j in range(1, 16):
        row_copy(j).wait_recv()

    def over(values):
        top = functools.reduce(jnp.maximum, values)
        return top + log2(functools.reduce(jnp.add, [jnp.exp2(v - top) for v in values]))

    rlse_s[...] = over([rowl_s[...]] + [rowl_r[j] for j in range(15)])
    clse_s[...] = over([coll_s[...]] + [coll_r[j] for j in range(7)])
    for q in range(8):
        crow_s[:, pl.ds(RANK[q] * 128, 128)] = clse_s[pl.ds(absolute(1, q), 1), :] + 1.0

    eye = (
        lax.broadcasted_iota(jnp.int32, (CHUNK, CHUNK), 0) == lax.broadcasted_iota(jnp.int32, (CHUNK, CHUNK), 1)
    )
    part_s[...] = jnp.zeros_like(part_s)

    def diagonal_slot(q, other):
        ix, iy, iz = (flipped[0][d] if q >> d & 1 else at[d] for d in range(3))
        ik = 1 - k if other else k
        tx, ty, tk, tz = iz, ix, iy // 2, lax.rem(iy, 2) * 2 + ik
        here = tk == k
        rank = 0
        for d, t in enumerate((tx, ty, tz)):
            across = t == flipped[1][d]
            here = here & (across | (t == at[d]))
            rank = rank + jnp.where(across, 1 << d, 0)
        rank = jnp.where(rank == 3, 4, jnp.where(rank == 4, 3, rank))
        return here, rank

    def column(row):
        return jnp.broadcast_to(row, (CHUNK, CHUNK)).T

    def grads(q, other):
        r = RANK[q] * 256 + other * CHUNK
        lse = column(rlse_s[pl.ds(row_index(q, other), 1), :] + 1.0)
        total = jnp.zeros((8, 128), F32)
        for j in range(8):
            u = u_s[pl.ds(r, CHUNK), pl.ds(j * 128, 128)]
            g = jnp.exp2(u - lse) + jnp.exp2(u - crow_s[:, pl.ds(j * 128, 128)])
            grad_s[pl.ds(r, CHUNK), pl.ds(j * 128, 128)] = g.astype(BF16)
            total = total + jnp.sum((g * u).reshape(16, 8, 128), axis=0)
        part_s[pl.ds(8, 8), :] += total
        here, rank = diagonal_slot(q, other)

        @pl.when(here)
        def _():
            at_col = pl.ds(pl.multiple_of(rank * 128, 128), 128)
            u = u_s[pl.ds(r, CHUNK), at_col]
            g = jnp.exp2(u - lse) + jnp.exp2(u - crow_s[:, at_col])
            grad_s[pl.ds(r, CHUNK), at_col] = jnp.where(eye, g - 1.0, g).astype(BF16)
            part_s[pl.ds(0, 8), :] += jnp.sum(jnp.where(eye, u, 0.0).reshape(16, 8, 128), axis=0)

    for q in range(8):
        for other in range(2):
            grads(q, other)
    diagonal = part_s[pl.ds(0, 8), :]
    part_s[pl.ds(8, 8), :] += -diagonal
    part_s[pl.ds(0, 8), :] = -2.0 * diagonal
    part_s[pl.ds(0, 1), :] += rlse_s[pl.ds(row_index(0, 0), 1), :] + clse_s[pl.ds(absolute(1, 0), 1), :]

    def total_copy(stage, j):
        if stage == 0:
            src, dst, device = part_s, part_r, place(0, j >> 1, j & 1)
        else:
            src, dst, device = part2_s, part2_r, place(1, j)
        i = j - 1 + 15 * stage
        return remote(src, dst.at[j - 1], tot_send.at[i], tot_recv.at[i], device)

    for j in range(1, 16):
        total_copy(0, j).start()

    def image_product(q):
        r = RANK[q] * 256
        for n in range(0, WIDTH, 256):
            acc = nn(grad_s[pl.ds(r, 256), :], txt[:, pl.ds(n, 256)])
            a_img[pl.ds(RANK[q] * CHUNK, CHUNK), pl.ds(n, 256)] = acc[0:CHUNK]
            core_s[pl.ds(q * CHUNK, CHUNK), pl.ds(n, 256)] = acc[CHUNK:].astype(BF16)
        sibling(q).start()

    def sibling(q):
        here = pl.ds(q * CHUNK, CHUNK)
        return remote(core_s.at[here], core_r.at[here], core_send.at[24 + q], core_recv.at[24 + q], place(0, 0, 1))

    def join_cores(q):
        sibling(q).wait_recv()
        here = pl.ds(RANK[q] * CHUNK, CHUNK)
        a_img[here, :] += core_r[pl.ds(q * CHUNK, CHUNK), :].astype(F32)

    def text_product(pair):
        for n in range(0, WIDTH, 256):
            acc = tn(grad_s[:, pl.ds(pair * 256, 256)], img[:, pl.ds(n, 256)])
            a_txt[pl.ds(pair * 256, 256), pl.ds(n, 256)] = acc

    def region(q, part, stage):
        kept = [p for p in range(8) if all(not p >> stage_dim(part, t) & 1 for t in range(stage, 3))]
        return {2: 0, 1: 4, 0: 6}[stage] + kept.index(q)

    def sum_copy(side, q, part):
        stage = last_stage(q, part)
        d = stage_dim(part, stage)
        start, rows = PARTS[part]
        to = region(q ^ (1 << d), part, stage)
        i = to * 3 + part
        return remote(
            rs_s.at[side, pl.ds(q * CHUNK + start, rows)], rs_r.at[side, pl.ds(to * CHUNK + start, rows)],
            rs_send.at[side, i], rs_recv.at[side, i], place(side, 1 << d),
        )

    def summed(side, q, part):
        start, rows = PARTS[part]
        acc = (a_img, a_txt)[side][pl.ds(RANK[q] * CHUNK + start, rows), :]
        for stage in range(2, last_stage(q, part), -1):
            d = stage_dim(part, stage)
            sum_copy(side, q | 1 << d, part).wait_recv()
            acc = acc + rs_r[side, pl.ds(region(q, part, stage) * CHUNK + start, rows), :].astype(F32)
        return acc

    def hand_on(side, q, part):
        start, rows = PARTS[part]
        rs_s[side, pl.ds(q * CHUNK + start, rows), :] = summed(side, q, part).astype(BF16)
        sum_copy(side, q, part).start()

    def rounds(side, slots, age):
        for q in slots:
            for part in range(3):
                if 2 - last_stage(q, part) == age:
                    hand_on(side, q, part)

    image_product(7)
    text_product(3)
    join_cores(7)
    rounds(0, (7,), 0)
    rounds(1, (7,), 0)
    rounds(1, (6,), 0)
    image_product(6)
    image_product(5)
    join_cores(6)
    rounds(0, (6,), 0)
    text_product(2)
    rounds(1, (5, 3), 0)
    join_cores(5)
    rounds(0, (5,), 0)
    image_product(3)
    image_product(4)
    join_cores(3)
    rounds(0, (3,), 0)
    rounds(0, (6, 5, 3), 1)
    rounds(1, (6, 5, 3), 1)
    join_cores(4)
    rounds(0, (4,), 0)
    text_product(1)
    rounds(1, (4, 2), 0)
    image_product(2)
    image_product(1)
    join_cores(2)
    rounds(0, (2,), 0)
    text_product(0)
    rounds(1, (1,), 0)
    join_cores(1)
    rounds(0, (1,), 0)
    rounds(0, (4, 2, 1), 1)
    rounds(1, (4, 2, 1), 1)
    image_product(0)
    for j in range(1, 16):
        total_copy(0, j).wait_recv()
    part2_s[...] = functools.reduce(jnp.add, [part_s[...]] + [part_r[j] for j in range(15)])
    for q in range(1, 8):
        total_copy(1, q).start()
    rounds(0, (4, 2, 1), 2)
    rounds(1, (4, 2, 1), 2)
    join_cores(0)

    for side, ref, out in ((0, image_ref, image_out), (1, text_ref, text_out)):
        for part, (start, rows) in enumerate(PARTS):
            here = pl.ds(start, rows)
            v = ref[here, :]
            inverse = lax.rsqrt(jnp.sum(v * v, axis=1, keepdims=True) + EPS)
            hat = v * inverse
            g = summed(side, 0, part) * scale
            out[here, :] = inverse * (g - hat * jnp.sum(hat * g, axis=1, keepdims=True))

    for q in range(1, 8):
        total_copy(1, q).wait_recv()
    totals = functools.reduce(jnp.add, [part2_s[...]] + [part2_r[j] for j in range(7)])
    pairs = 128.0 * CHUNK
    sums_out[0] = jnp.sum(totals[0:8]) * (LN2 / (2.0 * pairs))
    sums_out[1] = jnp.sum(totals[8:16]) * (LN2 / pairs)

    for side in range(2):
        for q in range(1, 8):
            for part in range(3):
                gather_copy(side, q, part).wait_send()
                sum_copy(side, q, part).wait_send()
    for q in range(8):
        sibling(q).wait_send()
        for part in range(3):
            core_copy(q, part).wait_send()
    for j in range(1, 16):
        row_copy(j).wait_send()
        total_copy(0, j).wait_send()
    for q in range(1, 8):
        col_copy(q).wait_send()
        total_copy(1, q).wait_send()


def local(image_features, text_features, logit_scale):
    vmem = pl.BlockSpec(memory_space=pltpu.VMEM)
    smem = pl.BlockSpec(memory_space=pltpu.SMEM)
    dma = pltpu.SemaphoreType.DMA
    image_grad, text_grad, sums = pl.pallas_call(
        kernel,
        out_shape=(
            jax.ShapeDtypeStruct((CHUNK, WIDTH), F32),
            jax.ShapeDtypeStruct((CHUNK, WIDTH), F32),
            jax.ShapeDtypeStruct((2,), F32),
        ),
        in_specs=[smem, vmem, vmem],
        out_specs=(vmem, vmem, smem),
        scratch_shapes=[
            pltpu.VMEM((2048, WIDTH), BF16),
            pltpu.VMEM((1024, WIDTH), BF16),
            pltpu.VMEM((2048, 1024), F32),
            pltpu.VMEM((2048, 1024), BF16),
            pltpu.VMEM((2048, 128), F32),
            pltpu.VMEM((2048, 128), F32),
            pltpu.VMEM((8, 1024), F32),
            pltpu.VMEM((8, 1024), F32),
            pltpu.VMEM((16, 128), F32),
            pltpu.VMEM((15, 16, 128), F32),
            pltpu.VMEM((8, 128), F32),
            pltpu.VMEM((7, 8, 128), F32),
            pltpu.VMEM((16, 128), F32),
            pltpu.VMEM((8, 128), F32),
            pltpu.VMEM((1, 1024), F32),
            pltpu.VMEM((1024, WIDTH), F32),
            pltpu.VMEM((1024, WIDTH), F32),
            pltpu.VMEM((1024, WIDTH), BF16),
            pltpu.VMEM((1024, WIDTH), BF16),
            pltpu.VMEM((2, 1024, WIDTH), BF16),
            pltpu.VMEM((2, 7 * CHUNK, WIDTH), BF16),
            pltpu.VMEM((16, 128), F32),
            pltpu.VMEM((15, 16, 128), F32),
            pltpu.VMEM((16, 128), F32),
            pltpu.VMEM((7, 16, 128), F32),
            dma((2, 21)),
            dma((2, 21)),
            dma((32,)),
            dma((32,)),
            dma((15,)),
            dma((15,)),
            dma((7,)),
            dma((7,)),
            dma((2, 21)),
            dma((2, 21)),
            dma((22,)),
            dma((22,)),
        ],
        compiler_params=pltpu.CompilerParams(
            collective_id=0, has_side_effects=True, vmem_limit_bytes=60 * 2**20
        ),
        name="contrastive",
    )(logit_scale, image_features, text_features)
    return sums[0:1], image_grad, text_grad, sums[1:2]


def solution(mesh):
    in_specs = (P(("row", "col"), None), P(("col", "row"), None), P())
    out_specs = (P(), P(("row", "col"), None), P(("col", "row"), None), P())
    return jax.shard_map(local, mesh=mesh, in_specs=in_specs, out_specs=out_specs, check_vma=False)
```

```python
import functools

import jax
import jax.numpy as jnp
from jax import lax
from jax.experimental import pallas as pl
from jax.experimental.pallas import tpu as pltpu
from jax.sharding import PartitionSpec as P

MESH = pl.DeviceIdType.MESH
EPS = 1e-06
LOG2E = 1.4426950408889634
LN2 = 0.6931471805599453
SHIFT = 34.0
TINY = 2.0**-60

CHUNK = 128
WIDTH = 1024
ORDER = (0, 1, 2, 4, 5, 3, 6, 7)
RANK = tuple(ORDER.index(q) for q in range(8))
PARTS = ((0, 48, 0, 896, 0), (48, 48, 0, 896, 1), (96, 32, 0, 1024, 2), (0, 96, 896, 128, 2))
N_PARTS = len(PARTS)
BF16 = jnp.bfloat16
F32 = jnp.float32


def stage_dim(part, stage):
    return (PARTS[part][4] + stage) % 3


def last_stage(q, part):
    stage = -1
    for t in range(3):
        if q >> stage_dim(part, t) & 1:
            stage = t
    return stage


def log2(x):
    return jnp.log(x) * LOG2E


def nt(a, b):
    return lax.dot_general(a, b, (((1,), (1,)), ((), ())), preferred_element_type=F32)


def nn(a, b):
    return lax.dot_general(a, b, (((1,), (0,)), ((), ())), preferred_element_type=F32)


def tn(a, b):
    return lax.dot_general(a, b, (((0,), (0,)), ((), ())), preferred_element_type=F32)


def flip_image(c):
    return c + 1 - 2 * lax.rem(c, 2)


def flip_text(c):
    return 3 - c


def kernel(
    scale_ref, image_ref, text_ref,
    image_out, text_out, sums_out,
    scale_s, feat_s, lse_s, eye_s,
    img, txt, u_s, grad_s, hi_s, lo_s, colhi_s, collo_s,
    rowl_s, rowl_r, coll_s, coll_r, rlse_s, clse_s, crow_s,
    a_img, a_txt, core_s, core_r, rs_s, rs_r,
    part_s, part_r, part2_s, part2_r,
    load_sem, ag_send, ag_recv, core_send, core_recv,
    lse_send, lse_recv, csum_send, csum_recv, rs_send, rs_recv, tot_send, tot_recv,
):
    z = lax.axis_index("row")
    c = lax.axis_index("col")
    x, y, k = c // 8, lax.rem(c // 2, 4), lax.rem(c, 2)
    at = (x, y, z)
    flipped = (tuple(flip_image(v) for v in at), tuple(flip_text(v) for v in at))

    def place(side, q, other_core=0):
        px, py, pz = (flipped[side][d] if q >> d & 1 else at[d] for d in range(3))
        return {"row": pz, "col": (px * 4 + py) * 2 + (1 - k if other_core else k)}

    def remote(src, dst, send, recv, device):
        return pltpu.make_async_remote_copy(
            src_ref=src, dst_ref=dst, send_sem=send, recv_sem=recv, device_id=device, device_id_type=MESH
        )

    loads = [
        pltpu.make_async_copy(image_ref, feat_s.at[0], load_sem.at[0]),
        pltpu.make_async_copy(text_ref, feat_s.at[1], load_sem.at[1]),
        pltpu.make_async_copy(scale_ref, scale_s, load_sem.at[2]),
    ]
    for load in loads:
        load.start()
    peers = [place(0, 0, 1)] + [place(side, 1 << d) for side in range(2) for d in range(3)]
    barrier = pltpu.get_barrier_semaphore()
    for peer in peers:
        pl.semaphore_signal(barrier, inc=1, device_id=peer, device_id_type=MESH)

    def normalized(side):
        v = feat_s[side]
        return v * lax.rsqrt(jnp.sum(v * v, axis=1, keepdims=True) + EPS)

    loads[0].wait()
    img[pl.ds(0, CHUNK), :] = normalized(0).astype(BF16)
    loads[1].wait()
    txt[pl.ds(0, CHUNK), :] = normalized(1).astype(BF16)
    loads[2].wait()
    scale = jnp.exp(jnp.full((8, 128), scale_s[0], F32))[0:1, 0:1]
    unit = scale * LOG2E
    hi_s[...] = jnp.zeros_like(hi_s)
    lo_s[...] = jnp.zeros_like(lo_s)
    colhi_s[...] = jnp.zeros_like(colhi_s)
    collo_s[...] = jnp.zeros_like(collo_s)

    eye = lax.broadcasted_iota(jnp.int32, (CHUNK, CHUNK), 0) == lax.broadcasted_iota(jnp.int32, (CHUNK, CHUNK), 1)
    eye_s[pl.ds(0, CHUNK), :] = jnp.zeros((CHUNK, CHUNK), F32)
    eye_s[pl.ds(CHUNK, CHUNK), :] = jnp.where(eye, 1.0, 0.0)
    pl.semaphore_wait(barrier, len(peers))

    def area(part, base):
        row, rows, col, cols, _ = PARTS[part]
        return pl.ds(base + row, rows), pl.ds(col, cols)

    def gather_rows(side, q, part):
        return (img, txt)[side].at[area(part, RANK[q] * (2 * CHUNK if side == 0 else CHUNK))]

    def gather_copy(side, q, part):
        d = stage_dim(part, last_stage(q, part))
        i = (q - 1) * N_PARTS + part
        return remote(
            gather_rows(side, q ^ (1 << d), part), gather_rows(side, q, part),
            ag_send.at[side, i], ag_recv.at[side, i], place(side, 1 << d),
        )

    def core_copy(q, part):
        base = RANK[q] * 2 * CHUNK
        i = q * N_PARTS + part
        return remote(
            img.at[area(part, base)], img.at[area(part, base + CHUNK)],
            core_send.at[i], core_recv.at[i], place(0, 0, 1),
        )

    def arrive(q, first, *dims):
        for part in range(N_PARTS):
            if PARTS[part][4] == first:
                for side in range(2):
                    gather_copy(side, q, part).wait_recv()
                    for d in dims:
                        gather_copy(side, q | 1 << d, part).start()
                core_copy(q, part).start()

    def send_on(q, first):
        for part in range(N_PARTS):
            if PARTS[part][4] == first:
                for side in range(2):
                    gather_copy(side, q, part).start()

    def both_cores(*slots):
        for q in slots:
            for part in range(N_PARTS):
                core_copy(q, part).wait_recv()

    for t in range(3):
        for d in range(3):
            send_on(1 << d, (d - t) % 3)
    for part in range(N_PARTS):
        core_copy(0, part).start()

    def scores(row0, rows, col0, cols):
        for r in range(row0, row0 + rows, 256):
            u = nt(img[pl.ds(r, 256), :], txt[pl.ds(col0, cols), :]) * unit
            u_s[pl.ds(r, 256), pl.ds(col0, cols)] = u
            hi = jnp.exp2(u - SHIFT)
            lo = jnp.exp2(jnp.minimum(u, 0.0) + SHIFT)
            for e, row_s, col_s in ((hi, hi_s, colhi_s), (lo, lo_s, collo_s)):
                row = e[:, 0:128]
                for j in range(1, cols // 128):
                    row = row + e[:, j * 128 : (j + 1) * 128]
                row_s[pl.ds(r, 256), :] += row
                col_s[:, pl.ds(col0, cols)] += jnp.sum(e.reshape(32, 8, cols), axis=0)

    def joined(hi, lo):
        return jnp.where(hi > TINY, log2(hi) + SHIFT, log2(lo) - SHIFT)

    def absolute(side, q):
        bits = [lax.rem(v, 2) for v in at] if side == 0 else [v // 2 for v in at]
        bits = [1 - b if q >> d & 1 else b for d, b in enumerate(bits)]
        return bits[0] + 2 * bits[1] + 4 * bits[2]

    def row_index(q, other):
        return absolute(0, q) * 2 + (1 - k if other else k)

    def row_sums(q):
        for other in range(2):
            r = RANK[q] * 256 + other * CHUNK
            hi = jnp.sum(hi_s[pl.ds(r, CHUNK), :].T, axis=0, keepdims=True)
            lo = jnp.sum(lo_s[pl.ds(r, CHUNK), :].T, axis=0, keepdims=True)
            rowl_s[pl.ds(row_index(q, other), 1), :] = joined(hi, lo)

    arrive(1, 0, 1, 2)
    arrive(4, 2, 0)
    arrive(2, 1, 2)
    arrive(1, 2, 1)
    arrive(2, 0, 2)
    arrive(4, 1, 0)
    send_on(3, 1)
    send_on(6, 2)
    arrive(1, 1)
    arrive(2, 2)
    arrive(4, 0)
    both_cores(0, 1, 2, 4)
    scores(0, 1024, 0, 512)
    arrive(5, 2, 1)
    arrive(3, 0, 2)
    arrive(5, 0)
    arrive(6, 1, 0)
    arrive(5, 1)
    both_cores(5)
    scores(1024, 256, 0, 512)
    scores(0, 1280, 512, 128)
    arrive(3, 2)
    arrive(3, 1)
    arrive(6, 2)
    arrive(6, 0)
    both_cores(3, 6)
    scores(1280, 512, 0, 512)
    scores(1280, 512, 512, 128)
    scores(0, 1792, 640, 256)
    for part in range(3):
        arrive(7, part)
    scores(0, 1792, 896, 128)
    for q in ORDER[:7]:
        row_sums(q)
    both_cores(7)
    scores(1792, 256, 0, 512)
    scores(1792, 256, 512, 512)

    row_sums(7)
    colsum = joined(
        jnp.sum(colhi_s[...], axis=0, keepdims=True), jnp.sum(collo_s[...], axis=0, keepdims=True)
    )
    for q in range(8):
        coll_s[pl.ds(absolute(1, q), 1), :] = colsum[:, RANK[q] * 128 : (RANK[q] + 1) * 128]

    part_s[...] = jnp.zeros_like(part_s)

    def matching(q, other):
        ix, iy, iz = (flipped[0][d] if q >> d & 1 else at[d] for d in range(3))
        ik = 1 - k if other else k
        tx, ty, tk, tz = iz, ix, iy // 2, lax.rem(iy, 2) * 2 + ik
        here = tk == k
        slot = 0
        for d, t in enumerate((tx, ty, tz)):
            across = t == flipped[1][d]
            here = here & (across | (t == at[d]))
            slot = slot + jnp.where(across, 1 << d, 0)
        rank = sum(jnp.where(slot == q, RANK[q], 0) for q in range(1, 8))
        return jnp.where(here, rank, -1)

    matches = [matching(q, other) for q in ORDER for other in range(2)]

    def row_copy(j):
        return remote(rowl_s, rowl_r.at[j - 1], lse_send.at[j - 1], lse_recv.at[j - 1], place(0, j >> 1, j & 1))

    def col_copy(q):
        return remote(coll_s, coll_r.at[q - 1], csum_send.at[q - 1], csum_recv.at[q - 1], place(1, q))

    for q in range(1, 8):
        col_copy(q).start()
    for j in range(1, 16):
        row_copy(j).start()
    for i, rank in enumerate(matches):

        @pl.when(rank >= 0)
        def _():
            u = u_s[pl.ds(i * CHUNK, CHUNK), pl.ds(pl.multiple_of(rank * 128, 128), 128)]
            own = u * eye_s[pl.ds(CHUNK, CHUNK), :]
            part_s[pl.ds(0, 8), :] += -2.0 * jnp.sum(own.reshape(16, 8, 128), axis=0)

    for q in range(1, 8):
        col_copy(q).wait_recv()
    for j in range(1, 16):
        row_copy(j).wait_recv()

    def over(values):
        top = functools.reduce(jnp.maximum, values)
        return top + log2(functools.reduce(jnp.add, [jnp.exp2(v - top) for v in values]))

    rlse_s[...] = over([rowl_s[...]] + [rowl_r[j] for j in range(15)])
    clse_s[...] = over([coll_s[...]] + [coll_r[j] for j in range(7)])
    for q in range(8):
        crow_s[:, pl.ds(RANK[q] * 128, 128)] = clse_s[pl.ds(absolute(1, q), 1), :] + 1.0

    def spread(rank):
        for other in range(2):
            lse = rlse_s[pl.ds(row_index(ORDER[rank], other), 1), :] + 1.0
            lse_s[pl.ds(rank * 256 + other * CHUNK, CHUNK), :] = jnp.broadcast_to(lse, (CHUNK, CHUNK)).T

    def grads(blocks):
        total = jnp.zeros((8, 128), F32)
        for i, j in blocks:
            for other in range(2):
                here = pl.ds(i * 256 + other * CHUNK, CHUNK)
                at_col = pl.ds(j * 128, 128)
                u = u_s[here, at_col]
                flag = jnp.where(matches[i * 2 + other] == j, CHUNK, 0)
                own = eye_s[pl.ds(pl.multiple_of(flag, CHUNK), CHUNK), :]
                g = jnp.exp2(u - lse_s[here, :]) + jnp.exp2(u - crow_s[:, at_col]) - own
                grad_s[here, at_col] = g.astype(BF16)
                total = total + jnp.sum((g * u).reshape(16, 8, 128), axis=0)
        part_s[pl.ds(8, 8), :] += total

    part_s[pl.ds(0, 1), :] += rlse_s[pl.ds(row_index(0, 0), 1), :] + clse_s[pl.ds(absolute(1, 0), 1), :]

    def total_copy(stage, j):
        if stage == 0:
            src, dst, device = part_s, part_r, place(0, j >> 1, j & 1)
        else:
            src, dst, device = part2_s, part2_r, place(1, j)
        i = j - 1 + 15 * stage
        return remote(src, dst.at[j - 1], tot_send.at[i], tot_recv.at[i], device)

    def row_blocks(rank):
        return [(rank, j) for j in range(rank + 1)]

    def col_blocks(rank):
        return [(i, rank) for i in range(rank)]

    def image_product(q):
        r = RANK[q] * 256
        for n in range(0, WIDTH, 256):
            acc = nn(grad_s[pl.ds(r, 256), :], txt[:, pl.ds(n, 256)])
            a_img[pl.ds(RANK[q] * CHUNK, CHUNK), pl.ds(n, 256)] = acc[0:CHUNK]
            core_s[pl.ds(q * CHUNK, CHUNK), pl.ds(n, 256)] = acc[CHUNK:].astype(BF16)

    def sibling(q):
        here = pl.ds(q * CHUNK, CHUNK)
        return remote(core_s.at[here], core_r.at[here], core_send.at[8 * N_PARTS + q], core_recv.at[8 * N_PARTS + q], place(0, 0, 1))

    def join_cores(q):
        sibling(q).wait_recv()
        here = pl.ds(RANK[q] * CHUNK, CHUNK)
        a_img[here, :] += core_r[pl.ds(q * CHUNK, CHUNK), :].astype(F32)

    def text_product(q):
        here = pl.ds(RANK[q] * CHUNK, CHUNK)
        for n in range(0, WIDTH, 256):
            a_txt[here, pl.ds(n, 256)] = tn(grad_s[:, here], img[:, pl.ds(n, 256)])

    def region(q, part, stage):
        kept = [p for p in range(8) if all(not p >> stage_dim(part, t) & 1 for t in range(stage, 3))]
        return {2: 0, 1: 4, 0: 6}[stage] + kept.index(q)

    def sum_copy(side, q, part):
        stage = last_stage(q, part)
        d = stage_dim(part, stage)
        to = region(q ^ (1 << d), part, stage)
        i = to * N_PARTS + part
        return remote(
            rs_s.at[(side, *area(part, q * CHUNK))], rs_r.at[(side, *area(part, to * CHUNK))],
            rs_send.at[side, i], rs_recv.at[side, i], place(side, 1 << d),
        )

    def summed(side, q, part):
        acc = (a_img, a_txt)[side][area(part, RANK[q] * CHUNK)]
        for stage in range(2, last_stage(q, part), -1):
            d = stage_dim(part, stage)
            sum_copy(side, q | 1 << d, part).wait_recv()
            acc = acc + rs_r[(side, *area(part, region(q, part, stage) * CHUNK))].astype(F32)
        return acc

    def hand_on(side, q, part):
        rs_s[(side, *area(part, q * CHUNK))] = summed(side, q, part).astype(BF16)
        sum_copy(side, q, part).start()

    def rounds(side, slots, age):
        for q in slots:
            for part in range(N_PARTS):
                if 2 - last_stage(q, part) == age:
                    hand_on(side, q, part)

    def image_step(q):
        image_product(q)
        sibling(q).start()

    def text_step(q):
        if q:
            grads(row_blocks(RANK[q] - 1) + col_blocks(RANK[q] - 1))
        text_product(q)
        rounds(1, (q,), 0)

    def join(q):
        join_cores(q)
        rounds(0, (q,), 0)

    spread(7)
    grads(row_blocks(7))
    image_step(7)
    for rank in range(6, -1, -1):
        spread(rank)
    grads(col_blocks(7))
    text_step(7)
    image_step(6)
    join(7)
    text_step(6)
    image_step(3)
    join(6)
    text_step(3)
    image_step(5)
    join(3)
    text_step(5)
    rounds(1, (6, 3, 5), 1)
    image_step(4)
    join(5)
    rounds(0, (6, 3, 5), 1)
    text_step(4)
    image_step(2)
    join(4)
    text_step(2)
    image_step(1)
    join(2)
    text_step(1)
    for j in range(1, 16):
        total_copy(0, j).start()
    rounds(1, (4, 2, 1), 1)
    image_step(0)
    join(1)
    rounds(0, (4, 2, 1), 1)
    text_step(0)
    rounds(1, (4, 2, 1), 2)
    rounds(0, (4, 2, 1), 2)
    for j in range(1, 16):
        total_copy(0, j).wait_recv()
    part2_s[...] = functools.reduce(jnp.add, [part_s[...]] + [part_r[j] for j in range(15)])
    for q in range(1, 8):
        total_copy(1, q).start()
    join_cores(0)

    for side, out in ((1, text_out), (0, image_out)):
        for part in range(N_PARTS):
            out[area(part, 0)] = summed(side, 0, part)
        for row in range(0, CHUNK, 32):
            here = pl.ds(row, 32)
            v = feat_s[side, here, :]
            inverse = lax.rsqrt(jnp.sum(v * v, axis=1, keepdims=True) + EPS)
            hat = v * inverse
            g = out[here, :] * scale
            out[here, :] = inverse * (g - hat * jnp.sum(hat * g, axis=1, keepdims=True))

    for q in range(1, 8):
        total_copy(1, q).wait_recv()
    totals = functools.reduce(jnp.add, [part2_s[...]] + [part2_r[j] for j in range(7)])
    pairs = 128.0 * CHUNK
    sums_out[0] = jnp.sum(totals[0:8]) * (LN2 / (2.0 * pairs))
    sums_out[1] = jnp.sum(totals[8:16]) * (LN2 / pairs)

    for side in range(2):
        for q in range(1, 8):
            for part in range(N_PARTS):
                gather_copy(side, q, part).wait_send()
                sum_copy(side, q, part).wait_send()
    for q in range(8):
        sibling(q).wait_send()
        for part in range(N_PARTS):
            core_copy(q, part).wait_send()
    for j in range(1, 16):
        row_copy(j).wait_send()
        total_copy(0, j).wait_send()
    for q in range(1, 8):
        col_copy(q).wait_send()
        total_copy(1, q).wait_send()


def deliver(image_ref, text_ref, sums_ref, loss_out, image_out, text_out, scale_out, sem):
    copies = [
        pltpu.make_async_copy(image_ref, image_out, sem.at[0]),
        pltpu.make_async_copy(text_ref, text_out, sem.at[1]),
    ]
    for copy in copies:
        copy.start()
    loss_out[0] = sums_ref[0]
    scale_out[0] = sums_ref[1]
    for copy in copies:
        copy.wait()


def local(image_features, text_features, logit_scale):
    hbm = pl.BlockSpec(memory_space=pltpu.HBM)
    vmem = pl.BlockSpec(memory_space=pltpu.VMEM)
    smem = pl.BlockSpec(memory_space=pltpu.SMEM)
    dma = pltpu.SemaphoreType.DMA
    image_grad, text_grad, sums = pl.pallas_call(
        kernel,
        out_shape=(
            pltpu.VMEM((CHUNK, WIDTH), F32),
            pltpu.VMEM((CHUNK, WIDTH), F32),
            pltpu.SMEM((2,), F32),
        ),
        in_specs=[hbm] * 3,
        out_specs=(vmem, vmem, smem),
        scratch_shapes=[
            pltpu.SMEM((1,), F32),
            pltpu.VMEM((2, CHUNK, WIDTH), F32),
            pltpu.VMEM((2048, 128), F32),
            pltpu.VMEM((2 * CHUNK, CHUNK), F32),
            pltpu.VMEM((2048, WIDTH), BF16),
            pltpu.VMEM((1024, WIDTH), BF16),
            pltpu.VMEM((2048, 1024), F32),
            pltpu.VMEM((2048, 1024), BF16),
            pltpu.VMEM((2048, 128), F32),
            pltpu.VMEM((2048, 128), F32),
            pltpu.VMEM((8, 1024), F32),
            pltpu.VMEM((8, 1024), F32),
            pltpu.VMEM((16, 128), F32),
            pltpu.VMEM((15, 16, 128), F32),
            pltpu.VMEM((8, 128), F32),
            pltpu.VMEM((7, 8, 128), F32),
            pltpu.VMEM((16, 128), F32),
            pltpu.VMEM((8, 128), F32),
            pltpu.VMEM((1, 1024), F32),
            pltpu.VMEM((1024, WIDTH), F32),
            pltpu.VMEM((1024, WIDTH), F32),
            pltpu.VMEM((1024, WIDTH), BF16),
            pltpu.VMEM((1024, WIDTH), BF16),
            pltpu.VMEM((2, 1024, WIDTH), BF16),
            pltpu.VMEM((2, 7 * CHUNK, WIDTH), BF16),
            pltpu.VMEM((16, 128), F32),
            pltpu.VMEM((15, 16, 128), F32),
            pltpu.VMEM((16, 128), F32),
            pltpu.VMEM((7, 16, 128), F32),
            dma((3,)),
            dma((2, 7 * N_PARTS)),
            dma((2, 7 * N_PARTS)),
            dma((8 * N_PARTS + 8,)),
            dma((8 * N_PARTS + 8,)),
            dma((15,)),
            dma((15,)),
            dma((7,)),
            dma((7,)),
            dma((2, 7 * N_PARTS)),
            dma((2, 7 * N_PARTS)),
            dma((22,)),
            dma((22,)),
        ],
        compiler_params=pltpu.CompilerParams(
            collective_id=0, has_side_effects=True, vmem_limit_bytes=60 * 2**20
        ),
        name="contrastive",
    )(logit_scale, image_features, text_features)
    one = jax.ShapeDtypeStruct((1,), F32)
    grad = jax.ShapeDtypeStruct((CHUNK, WIDTH), F32)
    return pl.pallas_call(
        deliver,
        out_shape=(one, grad, grad, one),
        in_specs=[vmem, vmem, smem],
        out_specs=(smem, hbm, hbm, smem),
        scratch_shapes=[dma((2,))],
        name="finish",
    )(image_grad, text_grad, sums)


def solution(mesh):
    in_specs = (P(("row", "col"), None), P(("col", "row"), None), P())
    out_specs = (P(), P(("row", "col"), None), P(("col", "row"), None), P())
    return jax.shard_map(local, mesh=mesh, in_specs=in_specs, out_specs=out_specs, check_vma=False)
```

```python
import functools

import jax
import jax.numpy as jnp
from jax import lax
from jax.experimental import pallas as pl
from jax.experimental.pallas import tpu as pltpu
from jax.sharding import PartitionSpec as P

MESH = pl.DeviceIdType.MESH
EPS = 1e-06
LOG2E = 1.4426950408889634
LN2 = 0.6931471805599453
SHIFT = 34.0
TINY = 2.0**-60

CHUNK = 128
WIDTH = 1024
ORDER = (0, 1, 2, 4, 5, 3, 6, 7)
RANK = tuple(ORDER.index(q) for q in range(8))
PARTS = ((0, 48, 0, 896, 0), (48, 48, 0, 896, 1), (96, 32, 0, 1024, 2), (0, 96, 896, 128, 2))
N_PARTS = 4
BF16 = jnp.bfloat16
F32 = jnp.float32


def stage_dim(part, stage):
    return (PARTS[part][4] + stage) % 3


def last_stage(q, part):
    stage = -1
    for t in range(3):
        if q >> stage_dim(part, t) & 1:
            stage = t
    return stage


def log2(x):
    return jnp.log(x) * LOG2E


def nt(a, b):
    return lax.dot_general(a, b, (((1,), (1,)), ((), ())), preferred_element_type=F32)


def nn(a, b):
    return lax.dot_general(a, b, (((1,), (0,)), ((), ())), preferred_element_type=F32)


def tn(a, b):
    return lax.dot_general(a, b, (((0,), (0,)), ((), ())), preferred_element_type=F32)


def flip_image(c):
    return c + 1 - 2 * lax.rem(c, 2)


def flip_text(c):
    return 3 - c


def kernel(
    scale_ref, image_ref, text_ref,
    loss_out, image_out, text_out, scale_out,
    scale_s, feat_s, lse_s, eye_s,
    img, txt, u_s, grad_s, flip_s, row_acc, col_acc, rowm_s, colm_s,
    rowl_s, rowl_r, coll_s, coll_r, rlse_s, clse_s, crow_s,
    a_img, a_txt, core_s, core_r, rs_s, rs_r,
    part_s, part_r, part2_s, part2_r, part3_s, part3_r,
    load_sem, ag_send, ag_recv, core_send, core_recv,
    lse_send, lse_recv, csum_send, csum_recv, rs_send, rs_recv, tot_send, tot_recv,
):
    z = lax.axis_index("row")
    c = lax.axis_index("col")
    x, y, k = c // 8, lax.rem(c // 2, 4), lax.rem(c, 2)
    at = (x, y, z)
    flipped = (tuple(flip_image(v) for v in at), tuple(flip_text(v) for v in at))

    def place(side, q, other_core=0):
        px, py, pz = (flipped[side][d] if q >> d & 1 else at[d] for d in range(3))
        return {"row": pz, "col": (px * 4 + py) * 2 + (1 - k if other_core else k)}

    def remote(src, dst, send, recv, device):
        return pltpu.make_async_remote_copy(
            src_ref=src, dst_ref=dst, send_sem=send, recv_sem=recv, device_id=device, device_id_type=MESH
        )

    loads = [
        pltpu.make_async_copy(image_ref, feat_s.at[0], load_sem.at[0]),
        pltpu.make_async_copy(text_ref, feat_s.at[1], load_sem.at[1]),
        pltpu.make_async_copy(scale_ref, scale_s, load_sem.at[2]),
    ]
    for load in loads:
        load.start()
    def taken(ref, sem):
        pltpu.make_async_copy(ref, ref, sem).wait()

    peers = [place(0, 0, 1)] + [place(side, 1 << d) for side in range(2) for d in range(3)]
    barrier = pltpu.get_barrier_semaphore()
    for peer in peers:
        pl.semaphore_signal(barrier, inc=1, device_id=peer, device_id_type=MESH)

    def normalized(side):
        v = feat_s[side]
        return v * lax.rsqrt(jnp.sum(v * v, axis=1, keepdims=True) + EPS)

    loads[0].wait()
    img[pl.ds(0, CHUNK), :] = normalized(0).astype(BF16)
    loads[1].wait()
    txt[pl.ds(0, CHUNK), :] = normalized(1).astype(BF16)
    loads[2].wait()
    scale = jnp.exp(jnp.full((8, 128), scale_s[0], F32))[0:1, 0:1]
    unit = scale * LOG2E
    row_acc[...] = jnp.zeros_like(row_acc)
    col_acc[...] = jnp.zeros_like(col_acc)

    eye = lax.broadcasted_iota(jnp.int32, (CHUNK, CHUNK), 0) == lax.broadcasted_iota(jnp.int32, (CHUNK, CHUNK), 1)
    eye_s[pl.ds(0, CHUNK), :] = jnp.zeros((CHUNK, CHUNK), F32)
    eye_s[pl.ds(CHUNK, CHUNK), :] = jnp.where(eye, 1.0, 0.0)
    pl.semaphore_wait(barrier, len(peers))

    def area(part, base):
        row, rows, col, cols, _ = PARTS[part]
        return pl.ds(base + row, rows), pl.ds(col, cols)

    def gather_rows(side, q, part):
        return (img, txt)[side].at[area(part, RANK[q] * (2 * CHUNK if side == 0 else CHUNK))]

    def gather_copy(side, q, part):
        d = stage_dim(part, last_stage(q, part))
        i = (q - 1) * N_PARTS + part
        return remote(
            gather_rows(side, q ^ (1 << d), part), gather_rows(side, q, part),
            ag_send.at[side], ag_recv.at[side, i], place(side, 1 << d),
        )

    def core_copy(q, part):
        base = RANK[q] * 2 * CHUNK
        return remote(
            img.at[area(part, base)], img.at[area(part, base + CHUNK)],
            core_send.at[0], core_recv.at[q], place(0, 0, 1),
        )

    def arrive(q, first, *dims):
        for part in range(N_PARTS):
            if PARTS[part][4] == first:
                for side in range(2):
                    gather_copy(side, q, part).wait_recv()
                    for d in dims:
                        gather_copy(side, q | 1 << d, part).start()
                core_copy(q, part).start()

    def send_on(q, first):
        for part in range(N_PARTS):
            if PARTS[part][4] == first:
                for side in range(2):
                    gather_copy(side, q, part).start()

    def both_cores(*slots):
        for q in slots:
            taken(img.at[pl.ds(RANK[q] * 256 + CHUNK, CHUNK)], core_recv.at[q])


    for t in range(3):
        for d in range(3):
            send_on(1 << d, (d - t) % 3)
    for part in range(N_PARTS):
        core_copy(0, part).start()

    def scores(row0, rows, col0, cols):
        for r in range(row0, row0 + rows, 256):
            u = nt(img[pl.ds(r, 256), :], txt[pl.ds(col0, cols), :]) * unit
            u_s[pl.ds(r, 256), pl.ds(col0, cols)] = u
            hi = jnp.exp2(u - SHIFT)
            lo = jnp.exp2(jnp.minimum(u, 0.0) + SHIFT)
            for i, e in enumerate((hi, lo, hi * u, lo * u)):
                row = e[:, 0:128]
                for j in range(1, cols // 128):
                    row = row + e[:, j * 128 : (j + 1) * 128]
                row_acc[i, pl.ds(r, 256), :] += row
                col_acc[i, :, pl.ds(col0, cols)] += jnp.sum(e.reshape(32, 8, cols), axis=0)

    def joined(hi, lo):
        return jnp.where(hi > TINY, log2(hi) + SHIFT, log2(lo) - SHIFT)

    def averaged(hi, lo, weighted_hi, weighted_lo):
        return jnp.where(hi > TINY, weighted_hi / hi, weighted_lo / lo)

    def absolute(side, q):
        bits = [lax.rem(v, 2) for v in at] if side == 0 else [v // 2 for v in at]
        bits = [1 - b if q >> d & 1 else b for d, b in enumerate(bits)]
        return bits[0] + 2 * bits[1] + 4 * bits[2]

    def row_index(q, other):
        return absolute(0, q) * 2 + (1 - k if other else k)

    def row_sums(q):
        for other in range(2):
            r = RANK[q] * 256 + other * CHUNK
            sums = [jnp.sum(row_acc[i, pl.ds(r, CHUNK), :].T, axis=0, keepdims=True) for i in range(4)]
            here = pl.ds(row_index(q, other), 1)
            rowl_s[here, :] = joined(*sums[:2])
            rowm_s[here, :] = averaged(*sums)

    arrive(1, 0, 1, 2)
    arrive(4, 2, 0)
    arrive(2, 1, 2)
    arrive(1, 2, 1)
    arrive(2, 0, 2)
    arrive(4, 1, 0)
    send_on(3, 1)
    send_on(6, 2)
    arrive(1, 1)
    arrive(2, 2)
    arrive(4, 0)
    both_cores(0, 1, 2, 4)
    scores(0, 1024, 0, 512)
    arrive(5, 2, 1)
    arrive(3, 0, 2)
    arrive(5, 0)
    arrive(6, 1, 0)
    arrive(5, 1)
    both_cores(5)
    scores(1024, 256, 0, 512)
    scores(0, 1280, 512, 128)
    arrive(3, 2)
    arrive(3, 1)
    arrive(6, 2)
    arrive(6, 0)
    both_cores(3, 6)
    scores(1280, 512, 0, 512)
    scores(1280, 512, 512, 128)
    scores(0, 1792, 640, 256)
    for part in range(3):
        arrive(7, part)

    def gathered():
        taken(img.at[pl.ds(0, 7 * CHUNK)], ag_send.at[0])
        taken(txt.at[pl.ds(0, 7 * CHUNK)], ag_send.at[1])
        taken(img.at[pl.ds(0, 8 * CHUNK)], core_send.at[0])
        taken(rowl_r, lse_send.at[0])
        taken(coll_r, csum_send.at[0])

    scores(0, 1792, 896, 128)
    for q in ORDER[:7]:
        row_sums(q)
    both_cores(7)
    scores(1792, 256, 0, 512)
    scores(1792, 256, 512, 512)

    row_sums(7)
    sums = [jnp.sum(col_acc[i], axis=0, keepdims=True) for i in range(4)]
    col_lse, col_mean = joined(*sums[:2]), averaged(*sums)
    for q in range(8):
        here, at_col = pl.ds(absolute(1, q), 1), slice(RANK[q] * 128, (RANK[q] + 1) * 128)
        coll_s[here, :] = col_lse[:, at_col]
        colm_s[here, :] = col_mean[:, at_col]
    part_s[...] = jnp.zeros_like(part_s)

    def matching(q, other):
        ix, iy, iz = (flipped[0][d] if q >> d & 1 else at[d] for d in range(3))
        ik = 1 - k if other else k
        tx, ty, tk, tz = iz, ix, iy // 2, lax.rem(iy, 2) * 2 + ik
        here = tk == k
        slot = 0
        for d, t in enumerate((tx, ty, tz)):
            across = t == flipped[1][d]
            here = here & (across | (t == at[d]))
            slot = slot + jnp.where(across, 1 << d, 0)
        rank = sum(jnp.where(slot == q, RANK[q], 0) for q in range(1, 8))
        return jnp.where(here, rank, -1)

    matches = [matching(q, other) for q in ORDER for other in range(2)]

    def row_copy(j):
        return remote(rowl_s, rowl_r.at[j - 1], lse_send.at[0], lse_recv.at[0], place(0, j >> 1, j & 1))

    def col_copy(q):
        return remote(coll_s, coll_r.at[q - 1], csum_send.at[0], csum_recv.at[0], place(1, q))

    for q in range(1, 8):
        col_copy(q).start()
    for j in range(1, 16):
        row_copy(j).start()
    for i, rank in enumerate(matches):

        @pl.when(rank >= 0)
        def _():
            u = u_s[pl.ds(i * CHUNK, CHUNK), pl.ds(pl.multiple_of(rank * 128, 128), 128)]
            own = u * eye_s[pl.ds(CHUNK, CHUNK), :]
            own = jnp.sum(own.reshape(16, 8, 128), axis=0)
            part_s[pl.ds(0, 8), :] += -2.0 * own
            part_s[pl.ds(8, 8), :] += -own

    taken(coll_r, csum_recv.at[0])
    taken(rowl_r, lse_recv.at[0])

    def over(values):
        top = functools.reduce(jnp.maximum, values)
        return top + log2(functools.reduce(jnp.add, [jnp.exp2(v - top) for v in values]))

    rlse_s[...] = over([rowl_s[...]] + [rowl_r[j] for j in range(15)])
    clse_s[...] = over([coll_s[...]] + [coll_r[j] for j in range(7)])
    for q in range(8):
        crow_s[:, pl.ds(RANK[q] * 128, 128)] = clse_s[pl.ds(absolute(1, q), 1), :] + 1.0

    def spread(rank):
        for other in range(2):
            lse = rlse_s[pl.ds(row_index(ORDER[rank], other), 1), :] + 1.0
            lse_s[pl.ds(rank * 256 + other * CHUNK, CHUNK), :] = jnp.broadcast_to(lse, (CHUNK, CHUNK)).T

    def grads(blocks):
        for i, j in blocks:
            for other in range(2):
                here = pl.ds(i * 256 + other * CHUNK, CHUNK)
                at_col = pl.ds(j * 128, 128)
                u = u_s[here, at_col]
                flag = jnp.where(matches[i * 2 + other] == j, CHUNK, 0)
                own = eye_s[pl.ds(pl.multiple_of(flag, CHUNK), CHUNK), :]
                g = jnp.exp2(u - lse_s[here, :]) + jnp.exp2(u - crow_s[:, at_col]) - own
                low = g.astype(BF16)
                grad_s[here, at_col] = low
                flip_s[at_col, here] = low.T

    weighted = jnp.exp2(rowl_s[...] - rlse_s[...]) * rowm_s[...]
    weighted = weighted[0:8] + weighted[8:16] + jnp.exp2(coll_s[...] - clse_s[...]) * colm_s[...]
    part_s[pl.ds(8, 8), :] += 0.5 * weighted
    part_s[pl.ds(0, 1), :] += rlse_s[pl.ds(row_index(0, 0), 1), :] + clse_s[pl.ds(absolute(1, 0), 1), :]

    def total_copy(stage, q):
        if stage == 0:
            return remote(part_s, part_r, tot_send.at[0], tot_recv.at[0], place(0, 0, 1))
        src, dst = ((part2_s, part2_r), (part3_s, part3_r))[stage - 1]
        return remote(src, dst.at[q - 1], tot_send.at[stage], tot_recv.at[stage], place(stage - 1, q))

    def row_blocks(rank):
        return [(rank, j) for j in range(rank + 1)]

    def col_blocks(rank):
        return [(i, rank) for i in range(rank)]

    def image_product(q):
        r = RANK[q] * 256
        for n in range(0, WIDTH, 256):
            acc = nn(grad_s[pl.ds(r, 256), :], txt[:, pl.ds(n, 256)])
            a_img[pl.ds(RANK[q] * CHUNK, CHUNK), pl.ds(n, 256)] = acc[0:CHUNK]
            core_s[pl.ds(q * CHUNK, CHUNK), pl.ds(n, 256)] = acc[CHUNK:].astype(BF16)

    def sibling(q):
        here = pl.ds(q * CHUNK, CHUNK)
        return remote(core_s.at[here], core_r.at[here], core_send.at[1], core_recv.at[8 + q], place(0, 0, 1))

    def text_product(q):
        here = pl.ds(RANK[q] * CHUNK, CHUNK)
        for n in range(0, WIDTH, 256):
            acc = nn(flip_s[here, :], img[:, pl.ds(n, 256)])
            a_txt[here, pl.ds(n, 256)] = acc
            if q:
                rs_s[1, pl.ds(q * CHUNK, CHUNK), pl.ds(n, 256)] = acc.astype(BF16)

    def region(q, part, stage):
        kept = [p for p in range(8) if all(not p >> stage_dim(part, t) & 1 for t in range(stage, 3))]
        return {2: 0, 1: 4, 0: 6}[stage] + kept.index(q)

    def sum_copy(side, q, part):
        stage = last_stage(q, part)
        d = stage_dim(part, stage)
        to = region(q ^ (1 << d), part, stage)
        i = to * N_PARTS + part
        return remote(
            rs_s.at[(side, *area(part, q * CHUNK))], rs_r.at[(side, *area(part, to * CHUNK))],
            rs_send.at[side], rs_recv.at[side, i], place(side, 1 << d),
        )

    def summed(side, q, part):
        acc = (a_img, a_txt)[side][area(part, RANK[q] * CHUNK)]
        if side == 0:
            acc = acc + core_r[area(part, q * CHUNK)].astype(F32)
        for stage in range(2, last_stage(q, part), -1):
            d = stage_dim(part, stage)
            sum_copy(side, q | 1 << d, part).wait_recv()
            acc = acc + rs_r[(side, *area(part, region(q, part, stage) * CHUNK))].astype(F32)
        return acc

    def hand_on(side, q, part):
        if not (side == 1 and last_stage(q, part) == 2):
            rs_s[(side, *area(part, q * CHUNK))] = summed(side, q, part).astype(BF16)
        sum_copy(side, q, part).start()

    def rounds(side, slots, age):
        for q in slots:
            for part in range(N_PARTS):
                if 2 - last_stage(q, part) == age:
                    hand_on(side, q, part)

    def join(q):
        sibling(q).wait_recv()

    def step(done, q):
        image_product(q)
        text_product(done)
        rank = RANK[q]
        if rank:
            grads(col_blocks(rank) + row_blocks(rank - 1))
        sibling(q).start()
        rounds(1, (done,), 0)
        join(done)
        rounds(0, (done,), 0)

    total_copy(0, 0).start()
    spread(7)
    grads(row_blocks(7))
    image_product(7)
    for rank in range(6, -1, -1):
        spread(rank)
    grads(col_blocks(7) + row_blocks(6))
    sibling(7).start()
    taken(part_r, tot_recv.at[0])
    part2_s[...] = part_s[...] + part_r[...]
    for q in range(1, 8):
        total_copy(1, q).start()
    step(7, 6)
    step(6, 3)
    taken(part2_r, tot_recv.at[1])
    part3_s[...] = functools.reduce(jnp.add, [part2_s[...]] + [part2_r[j] for j in range(7)])
    for q in range(1, 8):
        total_copy(2, q).start()
    step(3, 5)
    step(5, 4)
    rounds(1, (6, 3, 5), 1)
    rounds(0, (6, 3, 5), 1)
    step(4, 2)
    step(2, 1)
    rounds(1, (4,), 1)
    rounds(0, (4,), 1)
    step(1, 0)
    rounds(1, (2, 1), 1)
    rounds(0, (2, 1), 1)
    text_product(0)
    rounds(1, (4, 2, 1), 2)
    rounds(0, (4, 2, 1), 2)
    join(0)

    for side, out in ((1, text_out), (0, image_out)):
        for part in range(N_PARTS):
            out[area(part, 0)] = summed(side, 0, part)
        for row in range(0, CHUNK, 32):
            here = pl.ds(row, 32)
            v = feat_s[side, here, :]
            inverse = lax.rsqrt(jnp.sum(v * v, axis=1, keepdims=True) + EPS)
            hat = v * inverse
            g = out[here, :] * scale
            out[here, :] = inverse * (g - hat * jnp.sum(hat * g, axis=1, keepdims=True))

    taken(part3_r, tot_recv.at[2])
    totals = functools.reduce(jnp.add, [part3_s[...]] + [part3_r[j] for j in range(7)])
    pairs = 128.0 * CHUNK
    loss_out[0] = jnp.sum(totals[0:8]) * (LN2 / (2.0 * pairs))
    scale_out[0] = jnp.sum(totals[8:16]) * (LN2 / pairs)

    taken(rs_r.at[0], rs_send.at[0])
    taken(rs_r.at[1], rs_send.at[1])
    taken(core_s, core_send.at[1])
    taken(part_r, tot_send.at[0])
    taken(part2_r, tot_send.at[1])
    taken(part3_r, tot_send.at[2])
    gathered()


def local(image_features, text_features, logit_scale):
    hbm = pl.BlockSpec(memory_space=pltpu.HBM)
    vmem = pl.BlockSpec(memory_space=pltpu.VMEM)
    smem = pl.BlockSpec(memory_space=pltpu.SMEM)
    dma = pltpu.SemaphoreType.DMA
    results = pl.pallas_call(
        kernel,
        out_shape=(
            pltpu.SMEM((1,), F32),
            pltpu.VMEM((CHUNK, WIDTH), F32),
            pltpu.VMEM((CHUNK, WIDTH), F32),
            pltpu.SMEM((1,), F32),
        ),
        in_specs=[hbm] * 3,
        out_specs=(smem, vmem, vmem, smem),
        scratch_shapes=[
            pltpu.SMEM((1,), F32),
            pltpu.VMEM((2, CHUNK, WIDTH), F32),
            pltpu.VMEM((2048, 128), F32),
            pltpu.VMEM((2 * CHUNK, CHUNK), F32),
            pltpu.VMEM((2048, WIDTH), BF16),
            pltpu.VMEM((1024, WIDTH), BF16),
            pltpu.VMEM((2048, 1024), F32),
            pltpu.VMEM((2048, 1024), BF16),
            pltpu.VMEM((1024, 2048), BF16),
            pltpu.VMEM((4, 2048, 128), F32),
            pltpu.VMEM((4, 8, 1024), F32),
            pltpu.VMEM((16, 128), F32),
            pltpu.VMEM((8, 128), F32),
            pltpu.VMEM((16, 128), F32),
            pltpu.VMEM((15, 16, 128), F32),
            pltpu.VMEM((8, 128), F32),
            pltpu.VMEM((7, 8, 128), F32),
            pltpu.VMEM((16, 128), F32),
            pltpu.VMEM((8, 128), F32),
            pltpu.VMEM((1, 1024), F32),
            pltpu.VMEM((1024, WIDTH), F32),
            pltpu.VMEM((1024, WIDTH), F32),
            pltpu.VMEM((1024, WIDTH), BF16),
            pltpu.VMEM((1024, WIDTH), BF16),
            pltpu.VMEM((2, 1024, WIDTH), BF16),
            pltpu.VMEM((2, 7 * CHUNK, WIDTH), BF16),
            pltpu.VMEM((16, 128), F32),
            pltpu.VMEM((16, 128), F32),
            pltpu.VMEM((16, 128), F32),
            pltpu.VMEM((7, 16, 128), F32),
            pltpu.VMEM((16, 128), F32),
            pltpu.VMEM((7, 16, 128), F32),
            dma((3,)),
            dma((2,)),
            dma((2, 7 * N_PARTS)),
            dma((2,)),
            dma((16,)),
            dma((1,)),
            dma((1,)),
            dma((1,)),
            dma((1,)),
            dma((2,)),
            dma((2, 7 * N_PARTS)),
            dma((3,)),
            dma((3,)),
        ],
        compiler_params=pltpu.CompilerParams(
            collective_id=0, has_side_effects=True, vmem_limit_bytes=60 * 2**20
        ),
        name="contrastive",
    )(logit_scale, image_features, text_features)
    return results


def solution(mesh):
    in_specs = (P(("row", "col"), None), P(("col", "row"), None), P())
    out_specs = (P(), P(("row", "col"), None), P(("col", "row"), None), P())
    return jax.shard_map(local, mesh=mesh, in_specs=in_specs, out_specs=out_specs, check_vma=False)
```

```python
import functools

import jax
import jax.numpy as jnp
from jax import lax
from jax.experimental import pallas as pl
from jax.experimental.pallas import tpu as pltpu
from jax.sharding import PartitionSpec as P

MESH = pl.DeviceIdType.MESH
EPS = 1e-06
LOG2E = 1.4426950408889634
LN2 = 0.6931471805599453
SHIFT = 34.0
TINY = 2.0**-60

CHUNK = 128
WIDTH = 1024
ORDER = (0, 1, 2, 4, 5, 3, 6, 7)
RANK = tuple(ORDER.index(q) for q in range(8))
PARTS = ((0, 48, 0, 896, 0), (48, 48, 0, 896, 1), (96, 32, 0, 1024, 2), (0, 96, 896, 128, 2))
N_PARTS = 4
BF16 = jnp.bfloat16
F32 = jnp.float32


def stage_dim(part, stage):
    return (PARTS[part][4] + stage) % 3


def last_stage(q, part):
    stage = -1
    for t in range(3):
        if q >> stage_dim(part, t) & 1:
            stage = t
    return stage


def log2(x):
    return jnp.log(x) * LOG2E


def nt(a, b):
    return lax.dot_general(a, b, (((1,), (1,)), ((), ())), preferred_element_type=F32)


def nn(a, b):
    return lax.dot_general(a, b, (((1,), (0,)), ((), ())), preferred_element_type=F32)


def tn(a, b):
    return lax.dot_general(a, b, (((0,), (0,)), ((), ())), preferred_element_type=F32)


def flip_image(c):
    return c + 1 - 2 * lax.rem(c, 2)


def flip_text(c):
    return 3 - c


def kernel(
    scale_ref, image_ref, text_ref,
    loss_out, image_out, text_out, scale_out,
    scale_s, feat_s, lse_s, eye_s,
    img, txt, u_s, grad_s, flip_s, row_acc, col_acc, rows_s, cols_s,
    rowl_s, rowl_r, coll_s, coll_r, rlse_s, clse_s, crow_s,
    a_img, a_txt, core_s, core_r, rs_s, rs_r,
    part_s, part_r, part2_s, part2_r, part3_s, part3_r,
    load_sem, ag_send, ag_recv, core_send, core_recv,
    lse_send, lse_recv, csum_send, csum_recv, rs_send, rs_recv, tot_send, tot_recv,
):
    z = lax.axis_index("row")
    c = lax.axis_index("col")
    x, y, k = c // 8, lax.rem(c // 2, 4), lax.rem(c, 2)
    at = (x, y, z)
    flipped = (tuple(flip_image(v) for v in at), tuple(flip_text(v) for v in at))

    def place(side, q, other_core=0):
        px, py, pz = (flipped[side][d] if q >> d & 1 else at[d] for d in range(3))
        return {"row": pz, "col": (px * 4 + py) * 2 + (1 - k if other_core else k)}

    def remote(src, dst, send, recv, device):
        return pltpu.make_async_remote_copy(
            src_ref=src, dst_ref=dst, send_sem=send, recv_sem=recv, device_id=device, device_id_type=MESH
        )

    loads = [
        pltpu.make_async_copy(image_ref, feat_s.at[0], load_sem.at[0]),
        pltpu.make_async_copy(text_ref, feat_s.at[1], load_sem.at[1]),
        pltpu.make_async_copy(scale_ref, scale_s, load_sem.at[2]),
    ]
    for load in loads:
        load.start()
    def taken(ref, sem):
        pltpu.make_async_copy(ref, ref, sem).wait()

    peers = [place(0, 0, 1)] + [place(side, 1 << d) for side in range(2) for d in range(3)]
    barrier = pltpu.get_barrier_semaphore()
    for peer in peers:
        pl.semaphore_signal(barrier, inc=1, device_id=peer, device_id_type=MESH)

    def normalized(side):
        v = feat_s[side]
        return v * lax.rsqrt(jnp.sum(v * v, axis=1, keepdims=True) + EPS)

    loads[0].wait()
    img[pl.ds(0, CHUNK), :] = normalized(0).astype(BF16)
    loads[1].wait()
    txt[pl.ds(0, CHUNK), :] = normalized(1).astype(BF16)
    loads[2].wait()
    scale = jnp.exp(jnp.full((8, 128), scale_s[0], F32))[0:1, 0:1]
    unit = scale * LOG2E
    row_acc[...] = jnp.zeros_like(row_acc)
    col_acc[...] = jnp.zeros_like(col_acc)

    eye = lax.broadcasted_iota(jnp.int32, (CHUNK, CHUNK), 0) == lax.broadcasted_iota(jnp.int32, (CHUNK, CHUNK), 1)
    eye_s[pl.ds(0, CHUNK), :] = jnp.zeros((CHUNK, CHUNK), F32)
    eye_s[pl.ds(CHUNK, CHUNK), :] = jnp.where(eye, 1.0, 0.0)
    pl.semaphore_wait(barrier, len(peers))

    def area(part, base):
        row, rows, col, cols, _ = PARTS[part]
        return pl.ds(base + row, rows), pl.ds(col, cols)

    def gather_rows(side, q, part):
        return (img, txt)[side].at[area(part, RANK[q] * (2 * CHUNK if side == 0 else CHUNK))]

    def gather_copy(side, q, part):
        d = stage_dim(part, last_stage(q, part))
        i = (q - 1) * N_PARTS + part
        return remote(
            gather_rows(side, q ^ (1 << d), part), gather_rows(side, q, part),
            ag_send.at[side], ag_recv.at[side, i], place(side, 1 << d),
        )

    def core_copy(q, part):
        base = RANK[q] * 2 * CHUNK
        return remote(
            img.at[area(part, base)], img.at[area(part, base + CHUNK)],
            core_send.at[0], core_recv.at[q], place(0, 0, 1),
        )

    def arrive(q, first, *dims):
        for part in range(N_PARTS):
            if PARTS[part][4] == first:
                for side in range(2):
                    gather_copy(side, q, part).wait_recv()
                    for d in dims:
                        gather_copy(side, q | 1 << d, part).start()
                core_copy(q, part).start()

    def send_on(q, first):
        for part in range(N_PARTS):
            if PARTS[part][4] == first:
                for side in range(2):
                    gather_copy(side, q, part).start()

    def both_cores(*slots):
        for q in slots:
            taken(img.at[pl.ds(RANK[q] * 256 + CHUNK, CHUNK)], core_recv.at[q])


    for t in range(3):
        for d in range(3):
            send_on(1 << d, (d - t) % 3)
    for part in range(N_PARTS):
        core_copy(0, part).start()

    def scores(row0, rows, col0, cols):
        for r in range(row0, row0 + rows, 256):
            u = nt(img[pl.ds(r, 256), :], txt[pl.ds(col0, cols), :]) * unit
            u_s[pl.ds(r, 256), pl.ds(col0, cols)] = u
            hi = jnp.exp2(u - SHIFT)
            lo = jnp.exp2(jnp.minimum(u, 0.0) + SHIFT)
            for i, e in enumerate((hi, lo, hi * u, lo * u)):
                row = e[:, 0:128]
                for j in range(1, cols // 128):
                    row = row + e[:, j * 128 : (j + 1) * 128]
                row_acc[i, pl.ds(r, 256), :] += row
                col_acc[i, :, pl.ds(col0, cols)] += jnp.sum(e.reshape(32, 8, cols), axis=0)

    def joined(hi, lo):
        return jnp.where(hi > TINY, log2(hi) + SHIFT, log2(lo) - SHIFT)

    def averaged(hi, lo, weighted_hi, weighted_lo):
        return jnp.where(hi > TINY, weighted_hi / hi, weighted_lo / lo)

    def absolute(side, q):
        bits = [lax.rem(v, 2) for v in at] if side == 0 else [v // 2 for v in at]
        bits = [1 - b if q >> d & 1 else b for d, b in enumerate(bits)]
        return bits[0] + 2 * bits[1] + 4 * bits[2]

    def row_index(q, other):
        return absolute(0, q) * 2 + (1 - k if other else k)

    def row_sums(q, kinds):
        for other in range(2):
            for i in kinds:
                row = row_acc[i, pl.ds(RANK[q] * 256 + other * CHUNK, CHUNK), :]
                rows_s[i, pl.ds(row_index(q, other), 1), :] = jnp.sum(row.T, axis=0, keepdims=True)

    def col_sums(kinds):
        for i in kinds:
            row = jnp.sum(col_acc[i], axis=0, keepdims=True)
            for q in range(8):
                cols_s[i, pl.ds(absolute(1, q), 1), :] = row[:, RANK[q] * 128 : (RANK[q] + 1) * 128]

    arrive(1, 0, 1, 2)
    arrive(4, 2, 0)
    arrive(2, 1, 2)
    arrive(1, 2, 1)
    arrive(2, 0, 2)
    arrive(4, 1, 0)
    send_on(3, 1)
    send_on(6, 2)
    arrive(1, 1)
    arrive(2, 2)
    arrive(4, 0)
    both_cores(0, 1, 2, 4)
    scores(0, 1024, 0, 512)
    arrive(5, 2, 1)
    arrive(3, 0, 2)
    arrive(5, 0)
    arrive(6, 1, 0)
    arrive(5, 1)
    both_cores(5)
    scores(1024, 256, 0, 512)
    scores(0, 1280, 512, 128)
    arrive(3, 2)
    arrive(3, 1)
    arrive(6, 2)
    arrive(6, 0)
    both_cores(3, 6)
    scores(1280, 512, 0, 512)
    scores(1280, 512, 512, 128)
    scores(0, 1792, 640, 256)
    for part in range(3):
        arrive(7, part)

    def gathered():
        taken(img.at[pl.ds(0, 7 * CHUNK)], ag_send.at[0])
        taken(txt.at[pl.ds(0, 7 * CHUNK)], ag_send.at[1])
        taken(img.at[pl.ds(0, 8 * CHUNK)], core_send.at[0])
        taken(rowl_r, lse_send.at[0])
        taken(coll_r, csum_send.at[0])

    scores(0, 1792, 896, 128)
    for q in ORDER[:7]:
        row_sums(q, (0, 1))
    both_cores(7)
    scores(1792, 256, 0, 512)
    scores(1792, 256, 512, 512)

    def matching(q, other):
        ix, iy, iz = (flipped[0][d] if q >> d & 1 else at[d] for d in range(3))
        ik = 1 - k if other else k
        tx, ty, tk, tz = iz, ix, iy // 2, lax.rem(iy, 2) * 2 + ik
        here = tk == k
        slot = 0
        for d, t in enumerate((tx, ty, tz)):
            across = t == flipped[1][d]
            here = here & (across | (t == at[d]))
            slot = slot + jnp.where(across, 1 << d, 0)
        rank = sum(jnp.where(slot == q, RANK[q], 0) for q in range(1, 8))
        return jnp.where(here, rank, -1)


    def row_copy(j):
        return remote(rowl_s, rowl_r.at[j - 1], lse_send.at[0], lse_recv.at[0], place(0, j >> 1, j & 1))

    def col_copy(q):
        return remote(coll_s, coll_r.at[q - 1], csum_send.at[0], csum_recv.at[0], place(1, q))

    col_sums((0, 1))
    coll_s[...] = joined(cols_s[0], cols_s[1])
    for q in (7, 3, 5, 6, 1, 2, 4):
        col_copy(q).start()
    row_sums(7, (0, 1))
    rowl_s[...] = joined(rows_s[0], rows_s[1])
    for j in (15, 14, 13, 12, 11, 10, 7, 6, 9, 8, 5, 4, 3, 2, 1):
        row_copy(j).start()
    part_s[...] = jnp.zeros_like(part_s)
    col_sums((2, 3))
    for q in range(8):
        row_sums(q, (2, 3))
    matches = [matching(q, other) for q in ORDER for other in range(2)]
    for i, rank in enumerate(matches):

        @pl.when(rank >= 0)
        def _():
            u = u_s[pl.ds(i * CHUNK, CHUNK), pl.ds(pl.multiple_of(rank * 128, 128), 128)]
            own = u * eye_s[pl.ds(CHUNK, CHUNK), :]
            own = jnp.sum(own.reshape(16, 8, 128), axis=0)
            part_s[pl.ds(0, 8), :] += -2.0 * own
            part_s[pl.ds(8, 8), :] += -own

    taken(coll_r, csum_recv.at[0])
    taken(rowl_r, lse_recv.at[0])

    def over(values):
        top = functools.reduce(jnp.maximum, values)
        return top + log2(functools.reduce(jnp.add, [jnp.exp2(v - top) for v in values]))

    rlse_s[...] = over([rowl_s[...]] + [rowl_r[j] for j in range(15)])
    clse_s[...] = over([coll_s[...]] + [coll_r[j] for j in range(7)])
    for q in range(8):
        crow_s[:, pl.ds(RANK[q] * 128, 128)] = clse_s[pl.ds(absolute(1, q), 1), :] + 1.0

    def spread(rank):
        for other in range(2):
            lse = rlse_s[pl.ds(row_index(ORDER[rank], other), 1), :] + 1.0
            lse_s[pl.ds(rank * 256 + other * CHUNK, CHUNK), :] = jnp.broadcast_to(lse, (CHUNK, CHUNK)).T

    def grads(blocks):
        for i, j in blocks:
            for other in range(2):
                here = pl.ds(i * 256 + other * CHUNK, CHUNK)
                at_col = pl.ds(j * 128, 128)
                u = u_s[here, at_col]
                flag = jnp.where(matches[i * 2 + other] == j, CHUNK, 0)
                own = eye_s[pl.ds(pl.multiple_of(flag, CHUNK), CHUNK), :]
                g = jnp.exp2(u - lse_s[here, :]) + jnp.exp2(u - crow_s[:, at_col]) - own
                low = g.astype(BF16)
                grad_s[here, at_col] = low
                flip_s[at_col, here] = low.T

    weighted = jnp.exp2(rowl_s[...] - rlse_s[...]) * averaged(*(rows_s[i] for i in range(4)))
    weighted = weighted[0:8] + weighted[8:16] + jnp.exp2(coll_s[...] - clse_s[...]) * averaged(*(cols_s[i] for i in range(4)))
    part_s[pl.ds(8, 8), :] += 0.5 * weighted
    part_s[pl.ds(0, 1), :] += rlse_s[pl.ds(row_index(0, 0), 1), :] + clse_s[pl.ds(absolute(1, 0), 1), :]

    def total_copy(stage, q):
        if stage == 0:
            return remote(part_s, part_r, tot_send.at[0], tot_recv.at[0], place(0, 0, 1))
        src, dst = ((part2_s, part2_r), (part3_s, part3_r))[stage - 1]
        return remote(src, dst.at[q - 1], tot_send.at[stage], tot_recv.at[stage], place(stage - 1, q))

    def row_blocks(rank):
        return [(rank, j) for j in range(rank + 1)]

    def col_blocks(rank):
        return [(i, rank) for i in range(rank)]

    def image_product(q):
        r = RANK[q] * 256
        for n in range(0, WIDTH, 256):
            acc = nn(grad_s[pl.ds(r, 256), :], txt[:, pl.ds(n, 256)])
            a_img[pl.ds(RANK[q] * CHUNK, CHUNK), pl.ds(n, 256)] = acc[0:CHUNK]
            core_s[pl.ds(q * CHUNK, CHUNK), pl.ds(n, 256)] = acc[CHUNK:].astype(BF16)

    def sibling(q):
        here = pl.ds(q * CHUNK, CHUNK)
        return remote(core_s.at[here], core_r.at[here], core_send.at[1], core_recv.at[8 + q], place(0, 0, 1))

    def text_product(q):
        here = pl.ds(RANK[q] * CHUNK, CHUNK)
        for n in range(0, WIDTH, 256):
            acc = nn(flip_s[here, :], img[:, pl.ds(n, 256)])
            a_txt[here, pl.ds(n, 256)] = acc
            if q:
                rs_s[1, pl.ds(q * CHUNK, CHUNK), pl.ds(n, 256)] = acc.astype(BF16)

    def region(q, part, stage):
        kept = [p for p in range(8) if all(not p >> stage_dim(part, t) & 1 for t in range(stage, 3))]
        return {2: 0, 1: 4, 0: 6}[stage] + kept.index(q)

    def sum_copy(side, q, part):
        stage = last_stage(q, part)
        d = stage_dim(part, stage)
        to = region(q ^ (1 << d), part, stage)
        i = to * N_PARTS + part
        return remote(
            rs_s.at[(side, *area(part, q * CHUNK))], rs_r.at[(side, *area(part, to * CHUNK))],
            rs_send.at[side], rs_recv.at[side, i], place(side, 1 << d),
        )

    def summed(side, q, part):
        acc = (a_img, a_txt)[side][area(part, RANK[q] * CHUNK)]
        if side == 0:
            acc = acc + core_r[area(part, q * CHUNK)].astype(F32)
        for stage in range(2, last_stage(q, part), -1):
            d = stage_dim(part, stage)
            sum_copy(side, q | 1 << d, part).wait_recv()
            acc = acc + rs_r[(side, *area(part, region(q, part, stage) * CHUNK))].astype(F32)
        return acc

    def hand_on(side, q, part):
        if not (side == 1 and last_stage(q, part) == 2):
            rs_s[(side, *area(part, q * CHUNK))] = summed(side, q, part).astype(BF16)
        sum_copy(side, q, part).start()

    def rounds(side, slots, age):
        for q in slots:
            for part in range(N_PARTS):
                if 2 - last_stage(q, part) == age:
                    hand_on(side, q, part)

    def join(q):
        sibling(q).wait_recv()

    def step(done, q):
        image_product(q)
        text_product(done)
        rank = RANK[q]
        if rank:
            grads(col_blocks(rank) + row_blocks(rank - 1))
        sibling(q).start()
        rounds(1, (done,), 0)
        join(done)
        rounds(0, (done,), 0)

    def totals_1():
        taken(part_r, tot_recv.at[0])
        part2_s[...] = part_s[...] + part_r[...]
        for q in range(1, 8):
            total_copy(1, q).start()

    def totals_2():
        taken(part2_r, tot_recv.at[1])
        part3_s[...] = functools.reduce(jnp.add, [part2_s[...]] + [part2_r[j] for j in range(7)])
        for q in range(1, 8):
            total_copy(2, q).start()

    def corner(rank):
        grads(row_blocks(rank) + col_blocks(rank))

    def image_turn(q):
        image_product(q)
        sibling(q).start()

    def text_turn(q):
        text_product(q)
        rounds(1, (q,), 0)

    def join_turn(q):
        join(q)
        rounds(0, (q,), 0)

    total_copy(0, 0).start()
    for rank in range(7, -1, -1):
        spread(rank)
    corner(7)
    image_turn(7)
    text_turn(7)
    corner(6)
    image_turn(6)
    join_turn(7)
    text_turn(6)
    totals_1()
    corner(5)
    image_turn(3)
    join_turn(6)
    text_turn(3)
    corner(4)
    image_turn(5)
    join_turn(3)
    text_turn(5)
    totals_2()
    rounds(1, (6, 3, 5), 1)
    corner(3)
    image_turn(4)
    join_turn(5)
    rounds(0, (6, 3, 5), 1)
    text_turn(4)
    corner(2)
    image_turn(2)
    join_turn(4)
    text_turn(2)
    rounds(1, (4,), 1)
    corner(1)
    corner(0)
    image_turn(1)
    join_turn(2)
    rounds(0, (4,), 1)
    text_turn(1)
    rounds(1, (2, 1), 1)
    image_turn(0)
    join_turn(1)
    rounds(0, (2, 1), 1)
    text_product(0)
    rounds(1, (4, 2, 1), 2)
    rounds(0, (4, 2, 1), 2)
    join(0)

    for side, out in ((1, text_out), (0, image_out)):
        for part in range(N_PARTS):
            out[area(part, 0)] = summed(side, 0, part)
        for row in range(0, CHUNK, 32):
            here = pl.ds(row, 32)
            v = feat_s[side, here, :]
            inverse = lax.rsqrt(jnp.sum(v * v, axis=1, keepdims=True) + EPS)
            hat = v * inverse
            g = out[here, :] * scale
            out[here, :] = inverse * (g - hat * jnp.sum(hat * g, axis=1, keepdims=True))

    taken(part3_r, tot_recv.at[2])
    totals = functools.reduce(jnp.add, [part3_s[...]] + [part3_r[j] for j in range(7)])
    pairs = 128.0 * CHUNK
    loss_out[0] = jnp.sum(totals[0:8]) * (LN2 / (2.0 * pairs))
    scale_out[0] = jnp.sum(totals[8:16]) * (LN2 / pairs)

    taken(rs_r.at[0], rs_send.at[0])
    taken(rs_r.at[1], rs_send.at[1])
    taken(core_s, core_send.at[1])
    taken(part_r, tot_send.at[0])
    taken(part2_r, tot_send.at[1])
    taken(part3_r, tot_send.at[2])
    gathered()


def local(image_features, text_features, logit_scale):
    hbm = pl.BlockSpec(memory_space=pltpu.HBM)
    vmem = pl.BlockSpec(memory_space=pltpu.VMEM)
    smem = pl.BlockSpec(memory_space=pltpu.SMEM)
    dma = pltpu.SemaphoreType.DMA
    results = pl.pallas_call(
        kernel,
        out_shape=(
            pltpu.SMEM((1,), F32),
            pltpu.VMEM((CHUNK, WIDTH), F32),
            pltpu.VMEM((CHUNK, WIDTH), F32),
            pltpu.SMEM((1,), F32),
        ),
        in_specs=[hbm] * 3,
        out_specs=(smem, vmem, vmem, smem),
        scratch_shapes=[
            pltpu.SMEM((1,), F32),
            pltpu.VMEM((2, CHUNK, WIDTH), F32),
            pltpu.VMEM((2048, 128), F32),
            pltpu.VMEM((2 * CHUNK, CHUNK), F32),
            pltpu.VMEM((2048, WIDTH), BF16),
            pltpu.VMEM((1024, WIDTH), BF16),
            pltpu.VMEM((2048, 1024), F32),
            pltpu.VMEM((2048, 1024), BF16),
            pltpu.VMEM((1024, 2048), BF16),
            pltpu.VMEM((4, 2048, 128), F32),
            pltpu.VMEM((4, 8, 1024), F32),
            pltpu.VMEM((4, 16, 128), F32),
            pltpu.VMEM((4, 8, 128), F32),
            pltpu.VMEM((16, 128), F32),
            pltpu.VMEM((15, 16, 128), F32),
            pltpu.VMEM((8, 128), F32),
            pltpu.VMEM((7, 8, 128), F32),
            pltpu.VMEM((16, 128), F32),
            pltpu.VMEM((8, 128), F32),
            pltpu.VMEM((1, 1024), F32),
            pltpu.VMEM((1024, WIDTH), F32),
            pltpu.VMEM((1024, WIDTH), F32),
            pltpu.VMEM((1024, WIDTH), BF16),
            pltpu.VMEM((1024, WIDTH), BF16),
            pltpu.VMEM((2, 1024, WIDTH), BF16),
            pltpu.VMEM((2, 7 * CHUNK, WIDTH), BF16),
            pltpu.VMEM((16, 128), F32),
            pltpu.VMEM((16, 128), F32),
            pltpu.VMEM((16, 128), F32),
            pltpu.VMEM((7, 16, 128), F32),
            pltpu.VMEM((16, 128), F32),
            pltpu.VMEM((7, 16, 128), F32),
            dma((3,)),
            dma((2,)),
            dma((2, 7 * N_PARTS)),
            dma((2,)),
            dma((16,)),
            dma((1,)),
            dma((1,)),
            dma((1,)),
            dma((1,)),
            dma((2,)),
            dma((2, 7 * N_PARTS)),
            dma((3,)),
            dma((3,)),
        ],
        compiler_params=pltpu.CompilerParams(
            collective_id=0, has_side_effects=True, vmem_limit_bytes=60 * 2**20
        ),
        name="contrastive",
    )(logit_scale, image_features, text_features)
    return results


def solution(mesh):
    in_specs = (P(("row", "col"), None), P(("col", "row"), None), P())
    out_specs = (P(), P(("row", "col"), None), P(("col", "row"), None), P())
    return jax.shard_map(local, mesh=mesh, in_specs=in_specs, out_specs=out_specs, check_vma=False)
```

```python
import functools

import jax
import jax.numpy as jnp
from jax import lax
from jax.experimental import pallas as pl
from jax.experimental.pallas import tpu as pltpu
from jax.sharding import PartitionSpec as P

MESH = pl.DeviceIdType.MESH
EPS = 1e-06
LOG2E = 1.4426950408889634
LN2 = 0.6931471805599453
SHIFT = 34.0
TINY = 2.0**-60

CHUNK = 128
WIDTH = 1024
ORDER = (0, 1, 2, 4, 5, 3, 6, 7)
RANK = tuple(ORDER.index(q) for q in range(8))
PARTS = ((0, 48, 0, 896, 0), (48, 48, 0, 896, 1), (96, 32, 0, 1024, 2), (0, 96, 896, 128, 2))
N_PARTS = 4
BF16 = jnp.bfloat16
F32 = jnp.float32


def stage_dim(part, stage):
    return (PARTS[part][4] + stage) % 3


def last_stage(q, part):
    stage = -1
    for t in range(3):
        if q >> stage_dim(part, t) & 1:
            stage = t
    return stage


def log2(x):
    return jnp.log(x) * LOG2E


def nt(a, b):
    return lax.dot_general(a, b, (((1,), (1,)), ((), ())), preferred_element_type=F32)


def nn(a, b):
    return lax.dot_general(a, b, (((1,), (0,)), ((), ())), preferred_element_type=F32)


def tn(a, b):
    return lax.dot_general(a, b, (((0,), (0,)), ((), ())), preferred_element_type=F32)


def flip_image(c):
    return c + 1 - 2 * lax.rem(c, 2)


def flip_text(c):
    return 3 - c


def kernel(
    scale_ref, image_ref, text_ref,
    loss_out, image_out, text_out, scale_out,
    scale_s, feat_s, inv_s, lse_s, eye_s,
    img, txt, u_s, grad_s, flip_s, row_acc, col_acc, rows_s, cols_s,
    rowl_s, rowl_r, coll_s, coll_r, rlse_s, clse_s, crow_s,
    a_img, a_txt, core_s, core_r, rs_s, rs_r,
    part_s, part_r, part2_s, part2_r, part3_s, part3_r,
    load_sem, ag_send, ag_recv, core_send, core_recv,
    lse_send, lse_recv, csum_send, csum_recv, rs_send, rs_recv, tot_send, tot_recv,
):
    z = lax.axis_index("row")
    c = lax.axis_index("col")
    x, y, k = c // 8, lax.rem(c // 2, 4), lax.rem(c, 2)
    at = (x, y, z)
    flipped = (tuple(flip_image(v) for v in at), tuple(flip_text(v) for v in at))

    def place(side, q, other_core=0):
        px, py, pz = (flipped[side][d] if q >> d & 1 else at[d] for d in range(3))
        return {"row": pz, "col": (px * 4 + py) * 2 + (1 - k if other_core else k)}

    def remote(src, dst, send, recv, device):
        return pltpu.make_async_remote_copy(
            src_ref=src, dst_ref=dst, send_sem=send, recv_sem=recv, device_id=device, device_id_type=MESH
        )

    loads = [
        pltpu.make_async_copy(image_ref, feat_s.at[0], load_sem.at[0]),
        pltpu.make_async_copy(text_ref, feat_s.at[1], load_sem.at[1]),
        pltpu.make_async_copy(scale_ref, scale_s, load_sem.at[2]),
    ]
    for load in loads:
        load.start()
    def taken(ref, sem):
        pltpu.make_async_copy(ref, ref, sem).wait()

    peers = [place(0, 0, 1)] + [place(side, 1 << d) for side in range(2) for d in range(3)]
    barrier = pltpu.get_barrier_semaphore()
    for peer in peers:
        pl.semaphore_signal(barrier, inc=1, device_id=peer, device_id_type=MESH)

    def normalized(side):
        v = feat_s[side]
        return v * lax.rsqrt(jnp.sum(v * v, axis=1, keepdims=True) + EPS)

    loads[0].wait()
    img[pl.ds(0, CHUNK), :] = normalized(0).astype(BF16)
    loads[1].wait()
    txt[pl.ds(0, CHUNK), :] = normalized(1).astype(BF16)
    pl.semaphore_wait(barrier, len(peers))

    def area(part, base):
        row, rows, col, cols, _ = PARTS[part]
        return pl.ds(base + row, rows), pl.ds(col, cols)

    def gather_rows(side, q, part):
        return (img, txt)[side].at[area(part, RANK[q] * (2 * CHUNK if side == 0 else CHUNK))]

    def gather_copy(side, q, part):
        d = stage_dim(part, last_stage(q, part))
        i = (q - 1) * N_PARTS + part
        return remote(
            gather_rows(side, q ^ (1 << d), part), gather_rows(side, q, part),
            ag_send.at[side], ag_recv.at[side, i], place(side, 1 << d),
        )

    def core_copy(q, part):
        base = RANK[q] * 2 * CHUNK
        return remote(
            img.at[area(part, base)], img.at[area(part, base + CHUNK)],
            core_send.at[0], core_recv.at[q], place(0, 0, 1),
        )

    def arrive(q, first, *dims):
        for part in range(N_PARTS):
            if PARTS[part][4] == first:
                for side in range(2):
                    gather_copy(side, q, part).wait_recv()
                    for d in dims:
                        gather_copy(side, q | 1 << d, part).start()
                    if side == 0:
                        core_copy(q, part).start()

    def send_on(q, first):
        for part in range(N_PARTS):
            if PARTS[part][4] == first:
                for side in range(2):
                    gather_copy(side, q, part).start()

    def both_cores(*slots):
        for q in slots:
            taken(img.at[pl.ds(RANK[q] * 256 + CHUNK, CHUNK)], core_recv.at[q])


    for t in range(3):
        for d in range(3):
            send_on(1 << d, (d - t) % 3)
    for part in range(N_PARTS):
        core_copy(0, part).start()

    loads[2].wait()
    scale = jnp.exp(jnp.full((8, 128), scale_s[0], F32))[0:1, 0:1]
    unit = scale * LOG2E
    row_acc[...] = jnp.zeros_like(row_acc)
    col_acc[...] = jnp.zeros_like(col_acc)

    eye = lax.broadcasted_iota(jnp.int32, (CHUNK, CHUNK), 0) == lax.broadcasted_iota(jnp.int32, (CHUNK, CHUNK), 1)
    eye_s[pl.ds(0, CHUNK), :] = jnp.zeros((CHUNK, CHUNK), F32)
    eye_s[pl.ds(CHUNK, CHUNK), :] = jnp.where(eye, 1.0, 0.0)
    for side in range(2):
        v = feat_s[side]
        inverse = lax.rsqrt(jnp.sum(v * v, axis=1, keepdims=True) + EPS)
        feat_s[side] = v * inverse
        inv_s[side] = jnp.broadcast_to(inverse, (CHUNK, 128))

    def scores(row0, rows, col0, cols):
        for r in range(row0, row0 + rows, 256):
            u = nt(img[pl.ds(r, 256), :], txt[pl.ds(col0, cols), :]) * unit
            u_s[pl.ds(r, 256), pl.ds(col0, cols)] = u
            hi = jnp.exp2(u - SHIFT)
            lo = jnp.exp2(jnp.minimum(u, 0.0) + SHIFT)
            for i, e in enumerate((hi, lo, hi * u, lo * u)):
                row = e[:, 0:128]
                for j in range(1, cols // 128):
                    row = row + e[:, j * 128 : (j + 1) * 128]
                row_acc[i, pl.ds(r, 256), :] += row
                col_acc[i, :, pl.ds(col0, cols)] += jnp.sum(e.reshape(32, 8, cols), axis=0)

    def joined(hi, lo):
        return jnp.where(hi > TINY, log2(hi) + SHIFT, log2(lo) - SHIFT)

    def averaged(hi, lo, weighted_hi, weighted_lo):
        return jnp.where(hi > TINY, weighted_hi / hi, weighted_lo / lo)

    def absolute(side, q):
        bits = [lax.rem(v, 2) for v in at] if side == 0 else [v // 2 for v in at]
        bits = [1 - b if q >> d & 1 else b for d, b in enumerate(bits)]
        return bits[0] + 2 * bits[1] + 4 * bits[2]

    def row_index(q, other):
        return absolute(0, q) * 2 + (1 - k if other else k)

    def row_sums(q, kinds):
        for other in range(2):
            for i in kinds:
                row = row_acc[i, pl.ds(RANK[q] * 256 + other * CHUNK, CHUNK), :]
                rows_s[i, pl.ds(row_index(q, other), 1), :] = jnp.sum(row.T, axis=0, keepdims=True)

    def col_sums(kinds):
        for i in kinds:
            row = jnp.sum(col_acc[i], axis=0, keepdims=True)
            for q in range(8):
                cols_s[i, pl.ds(absolute(1, q), 1), :] = row[:, RANK[q] * 128 : (RANK[q] + 1) * 128]

    arrive(1, 0, 1, 2)
    arrive(4, 2, 0)
    arrive(2, 1, 2)
    arrive(1, 2, 1)
    arrive(2, 0, 2)
    arrive(4, 1, 0)
    send_on(3, 1)
    send_on(6, 2)
    arrive(1, 1)
    arrive(2, 2)
    arrive(4, 0)
    both_cores(0, 1, 2, 4)
    scores(0, 1024, 0, 512)
    arrive(5, 2, 1)
    arrive(3, 0, 2)
    arrive(5, 0)
    arrive(6, 1, 0)
    arrive(5, 1)
    both_cores(5)
    scores(1024, 256, 0, 512)
    scores(0, 1280, 512, 128)
    arrive(3, 2)
    arrive(3, 1)
    arrive(6, 2)
    arrive(6, 0)
    both_cores(3, 6)
    scores(1280, 512, 0, 512)
    scores(1280, 512, 512, 128)
    scores(0, 1792, 640, 256)
    for part in range(3):
        arrive(7, part)

    def gathered():
        taken(img.at[pl.ds(0, 7 * CHUNK)], ag_send.at[0])
        taken(txt.at[pl.ds(0, 7 * CHUNK)], ag_send.at[1])
        taken(img.at[pl.ds(0, 8 * CHUNK)], core_send.at[0])
        taken(rowl_r, lse_send.at[0])
        taken(coll_r, csum_send.at[0])

    scores(0, 1792, 896, 128)
    for q in ORDER[:7]:
        row_sums(q, (0, 1))
    both_cores(7)
    scores(1792, 256, 0, 512)
    scores(1792, 256, 512, 512)

    def matching(q, other):
        ix, iy, iz = (flipped[0][d] if q >> d & 1 else at[d] for d in range(3))
        ik = 1 - k if other else k
        tx, ty, tk, tz = iz, ix, iy // 2, lax.rem(iy, 2) * 2 + ik
        here = tk == k
        slot = 0
        for d, t in enumerate((tx, ty, tz)):
            across = t == flipped[1][d]
            here = here & (across | (t == at[d]))
            slot = slot + jnp.where(across, 1 << d, 0)
        rank = sum(jnp.where(slot == q, RANK[q], 0) for q in range(1, 8))
        return jnp.where(here, rank, -1)


    def row_copy(j):
        return remote(rowl_s, rowl_r.at[j - 1], lse_send.at[0], lse_recv.at[0], place(0, j >> 1, j & 1))

    def col_copy(q):
        return remote(coll_s, coll_r.at[q - 1], csum_send.at[0], csum_recv.at[0], place(1, q))

    col_sums((0, 1))
    coll_s[...] = joined(cols_s[0], cols_s[1])
    for q in (7, 3, 5, 6, 1, 2, 4):
        col_copy(q).start()
    row_sums(7, (0, 1))
    rowl_s[...] = joined(rows_s[0], rows_s[1])
    for j in (15, 14, 13, 12, 11, 10, 7, 6, 9, 8, 5, 4, 3, 2, 1):
        row_copy(j).start()
    part_s[...] = jnp.zeros_like(part_s)
    col_sums((2, 3))
    for q in range(8):
        row_sums(q, (2, 3))
    matches = [matching(q, other) for q in ORDER for other in range(2)]
    for i, rank in enumerate(matches):

        @pl.when(rank >= 0)
        def _():
            u = u_s[pl.ds(i * CHUNK, CHUNK), pl.ds(pl.multiple_of(rank * 128, 128), 128)]
            own = u * eye_s[pl.ds(CHUNK, CHUNK), :]
            own = jnp.sum(own.reshape(16, 8, 128), axis=0)
            part_s[pl.ds(0, 8), :] += -2.0 * own
            part_s[pl.ds(8, 8), :] += -own

    taken(coll_r, csum_recv.at[0])
    taken(rowl_r, lse_recv.at[0])

    def over(values):
        top = functools.reduce(jnp.maximum, values)
        return top + log2(functools.reduce(jnp.add, [jnp.exp2(v - top) for v in values]))

    rlse_s[...] = over([rowl_s[...]] + [rowl_r[j] for j in range(15)])
    clse_s[...] = over([coll_s[...]] + [coll_r[j] for j in range(7)])
    for q in range(8):
        crow_s[:, pl.ds(RANK[q] * 128, 128)] = clse_s[pl.ds(absolute(1, q), 1), :] + 1.0

    def spread(rank):
        for other in range(2):
            lse = rlse_s[pl.ds(row_index(ORDER[rank], other), 1), :] + 1.0
            lse_s[pl.ds(rank * 256 + other * CHUNK, CHUNK), :] = jnp.broadcast_to(lse, (CHUNK, CHUNK)).T

    def grads(blocks):
        for i, j in blocks:
            for other in range(2):
                here = pl.ds(i * 256 + other * CHUNK, CHUNK)
                at_col = pl.ds(j * 128, 128)
                u = u_s[here, at_col]
                flag = jnp.where(matches[i * 2 + other] == j, CHUNK, 0)
                own = eye_s[pl.ds(pl.multiple_of(flag, CHUNK), CHUNK), :]
                g = jnp.exp2(u - lse_s[here, :]) + jnp.exp2(u - crow_s[:, at_col]) - own
                low = g.astype(BF16)
                grad_s[here, at_col] = low
                flip_s[at_col, here] = low.T

    weighted = jnp.exp2(rowl_s[...] - rlse_s[...]) * averaged(*(rows_s[i] for i in range(4)))
    weighted = weighted[0:8] + weighted[8:16] + jnp.exp2(coll_s[...] - clse_s[...]) * averaged(*(cols_s[i] for i in range(4)))
    part_s[pl.ds(8, 8), :] += 0.5 * weighted
    part_s[pl.ds(0, 1), :] += rlse_s[pl.ds(row_index(0, 0), 1), :] + clse_s[pl.ds(absolute(1, 0), 1), :]

    def total_copy(stage, q):
        if stage == 0:
            return remote(part_s, part_r, tot_send.at[0], tot_recv.at[0], place(0, 0, 1))
        src, dst = ((part2_s, part2_r), (part3_s, part3_r))[stage - 1]
        return remote(src, dst.at[q - 1], tot_send.at[stage], tot_recv.at[stage], place(stage - 1, q))

    def row_blocks(rank):
        return [(rank, j) for j in range(rank + 1)]

    def col_blocks(rank):
        return [(i, rank) for i in range(rank)]

    def image_product(q):
        r = RANK[q] * 256
        for n in range(0, WIDTH, 256):
            acc = nn(grad_s[pl.ds(r, 256), :], txt[:, pl.ds(n, 256)])
            a_img[pl.ds(RANK[q] * CHUNK, CHUNK), pl.ds(n, 256)] = acc[0:CHUNK]
            core_s[pl.ds(q * CHUNK, CHUNK), pl.ds(n, 256)] = acc[CHUNK:].astype(BF16)

    def sibling(q):
        here = pl.ds(q * CHUNK, CHUNK)
        return remote(core_s.at[here], core_r.at[here], core_send.at[1], core_recv.at[8 + q], place(0, 0, 1))

    def text_product(q):
        here = pl.ds(RANK[q] * CHUNK, CHUNK)
        for n in range(0, WIDTH, 256):
            acc = nn(flip_s[here, :], img[:, pl.ds(n, 256)])
            a_txt[here, pl.ds(n, 256)] = acc
            if q:
                rs_s[1, pl.ds(q * CHUNK, CHUNK), pl.ds(n, 256)] = acc.astype(BF16)

    def region(q, part, stage):
        kept = [p for p in range(8) if all(not p >> stage_dim(part, t) & 1 for t in range(stage, 3))]
        return {2: 0, 1: 4, 0: 6}[stage] + kept.index(q)

    def sum_copy(side, q, part):
        stage = last_stage(q, part)
        d = stage_dim(part, stage)
        to = region(q ^ (1 << d), part, stage)
        i = to * N_PARTS + part
        return remote(
            rs_s.at[(side, *area(part, q * CHUNK))], rs_r.at[(side, *area(part, to * CHUNK))],
            rs_send.at[side], rs_recv.at[side, i], place(side, 1 << d),
        )

    def received(side, q, part, stage):
        sum_copy(side, q | 1 << stage_dim(part, stage), part).wait_recv()
        return rs_r[(side, *area(part, region(q, part, stage) * CHUNK))].astype(F32)

    def summed(side, q, part, upto):
        acc = (a_img, a_txt)[side][area(part, RANK[q] * CHUNK)]
        if side == 0:
            acc = acc + core_r[area(part, q * CHUNK)].astype(F32)
        for stage in range(2, upto, -1):
            acc = acc + received(side, q, part, stage)
        return acc

    def hand_on(side, q, part):
        if not (side == 1 and last_stage(q, part) == 2):
            rs_s[(side, *area(part, q * CHUNK))] = summed(side, q, part, last_stage(q, part)).astype(BF16)
        sum_copy(side, q, part).start()

    def rounds(side, slots, age):
        for q in slots:
            for part in range(N_PARTS):
                if 2 - last_stage(q, part) == age:
                    hand_on(side, q, part)

    def join(q):
        sibling(q).wait_recv()

    def step(done, q):
        image_product(q)
        text_product(done)
        rank = RANK[q]
        if rank:
            grads(col_blocks(rank) + row_blocks(rank - 1))
        sibling(q).start()
        rounds(1, (done,), 0)
        join(done)
        rounds(0, (done,), 0)

    def totals_1():
        taken(part_r, tot_recv.at[0])
        part2_s[...] = part_s[...] + part_r[...]
        for q in range(1, 8):
            total_copy(1, q).start()

    def totals_2():
        taken(part2_r, tot_recv.at[1])
        part3_s[...] = functools.reduce(jnp.add, [part2_s[...]] + [part2_r[j] for j in range(7)])
        for q in range(1, 8):
            total_copy(2, q).start()

    def corner(rank):
        grads(row_blocks(rank) + col_blocks(rank))

    def image_turn(q):
        image_product(q)
        sibling(q).start()

    def text_turn(q):
        text_product(q)
        rounds(1, (q,), 0)

    def join_turn(q):
        join(q)
        rounds(0, (q,), 0)

    total_copy(0, 0).start()
    for rank in range(7, -1, -1):
        spread(rank)
    corner(7)
    image_turn(7)
    text_turn(7)
    corner(6)
    image_turn(6)
    join_turn(7)
    text_turn(6)
    totals_1()
    corner(5)
    image_turn(3)
    join_turn(6)
    text_turn(3)
    corner(4)
    image_turn(5)
    join_turn(3)
    text_turn(5)
    totals_2()
    rounds(1, (6, 3, 5), 1)
    corner(3)
    image_turn(4)
    join_turn(5)
    rounds(0, (6, 3, 5), 1)
    text_turn(4)
    corner(2)
    image_turn(2)
    join_turn(4)
    text_turn(2)
    rounds(1, (4,), 1)
    corner(1)
    corner(0)
    image_turn(1)
    join_turn(2)
    rounds(0, (4,), 1)
    text_turn(1)
    rounds(1, (2, 1), 1)
    image_turn(0)
    join_turn(1)
    rounds(0, (2, 1), 1)
    text_product(0)
    rounds(1, (4, 2, 1), 2)
    rounds(0, (4, 2, 1), 2)
    join(0)

    outs = (image_out, text_out)
    for side in (1, 0):
        for part in range(N_PARTS):
            outs[side][area(part, 0)] = summed(side, 0, part, 0)
    for side in (1, 0):
        for part in range(N_PARTS):
            outs[side][area(part, 0)] += received(side, 0, part, 0)
        hat, g = feat_s[side], outs[side][...] * scale
        inverse = inv_s[side][:, 0:1]
        outs[side][...] = inverse * (g - hat * jnp.sum(hat * g, axis=1, keepdims=True))

    taken(part3_r, tot_recv.at[2])
    totals = functools.reduce(jnp.add, [part3_s[...]] + [part3_r[j] for j in range(7)])
    pairs = 128.0 * CHUNK
    loss_out[0] = jnp.sum(totals[0:8]) * (LN2 / (2.0 * pairs))
    scale_out[0] = jnp.sum(totals[8:16]) * (LN2 / pairs)

    taken(rs_r.at[0], rs_send.at[0])
    taken(rs_r.at[1], rs_send.at[1])
    taken(core_s, core_send.at[1])
    taken(part_r, tot_send.at[0])
    taken(part2_r, tot_send.at[1])
    taken(part3_r, tot_send.at[2])
    gathered()


def local(image_features, text_features, logit_scale):
    hbm = pl.BlockSpec(memory_space=pltpu.HBM)
    vmem = pl.BlockSpec(memory_space=pltpu.VMEM)
    smem = pl.BlockSpec(memory_space=pltpu.SMEM)
    dma = pltpu.SemaphoreType.DMA
    results = pl.pallas_call(
        kernel,
        out_shape=(
            pltpu.SMEM((1,), F32),
            pltpu.VMEM((CHUNK, WIDTH), F32),
            pltpu.VMEM((CHUNK, WIDTH), F32),
            pltpu.SMEM((1,), F32),
        ),
        in_specs=[hbm] * 3,
        out_specs=(smem, vmem, vmem, smem),
        scratch_shapes=[
            pltpu.SMEM((1,), F32),
            pltpu.VMEM((2, CHUNK, WIDTH), F32),
            pltpu.VMEM((2, CHUNK, 128), F32),
            pltpu.VMEM((2048, 128), F32),
            pltpu.VMEM((2 * CHUNK, CHUNK), F32),
            pltpu.VMEM((2048, WIDTH), BF16),
            pltpu.VMEM((1024, WIDTH), BF16),
            pltpu.VMEM((2048, 1024), F32),
            pltpu.VMEM((2048, 1024), BF16),
            pltpu.VMEM((1024, 2048), BF16),
            pltpu.VMEM((4, 2048, 128), F32),
            pltpu.VMEM((4, 8, 1024), F32),
            pltpu.VMEM((4, 16, 128), F32),
            pltpu.VMEM((4, 8, 128), F32),
            pltpu.VMEM((16, 128), F32),
            pltpu.VMEM((15, 16, 128), F32),
            pltpu.VMEM((8, 128), F32),
            pltpu.VMEM((7, 8, 128), F32),
            pltpu.VMEM((16, 128), F32),
            pltpu.VMEM((8, 128), F32),
            pltpu.VMEM((1, 1024), F32),
            pltpu.VMEM((1024, WIDTH), F32),
            pltpu.VMEM((1024, WIDTH), F32),
            pltpu.VMEM((1024, WIDTH), BF16),
            pltpu.VMEM((1024, WIDTH), BF16),
            pltpu.VMEM((2, 1024, WIDTH), BF16),
            pltpu.VMEM((2, 7 * CHUNK, WIDTH), BF16),
            pltpu.VMEM((16, 128), F32),
            pltpu.VMEM((16, 128), F32),
            pltpu.VMEM((16, 128), F32),
            pltpu.VMEM((7, 16, 128), F32),
            pltpu.VMEM((16, 128), F32),
            pltpu.VMEM((7, 16, 128), F32),
            dma((3,)),
            dma((2,)),
            dma((2, 7 * N_PARTS)),
            dma((2,)),
            dma((16,)),
            dma((1,)),
            dma((1,)),
            dma((1,)),
            dma((1,)),
            dma((2,)),
            dma((2, 7 * N_PARTS)),
            dma((3,)),
            dma((3,)),
        ],
        compiler_params=pltpu.CompilerParams(
            collective_id=0, has_side_effects=True, vmem_limit_bytes=60 * 2**20
        ),
        name="contrastive",
    )(logit_scale, image_features, text_features)
    return results


def solution(mesh):
    in_specs = (P(("row", "col"), None), P(("col", "row"), None), P())
    out_specs = (P(), P(("row", "col"), None), P(("col", "row"), None), P())
    return jax.shard_map(local, mesh=mesh, in_specs=in_specs, out_specs=out_specs, check_vma=False)
```

```python
import functools

import jax
import jax.numpy as jnp
from jax import lax
from jax.experimental import pallas as pl
from jax.experimental.pallas import tpu as pltpu
from jax.sharding import PartitionSpec as P

MESH = pl.DeviceIdType.MESH
EPS = 1e-06
LOG2E = 1.4426950408889634
LN2 = 0.6931471805599453
SHIFT = 34.0
TINY = 2.0**-60

CHUNK = 128
WIDTH = 1024
ORDER = (0, 1, 2, 4, 5, 3, 6, 7)
RANK = tuple(ORDER.index(q) for q in range(8))
PARTS = ((0, 48, 0, 896, 0), (48, 48, 0, 896, 1), (96, 32, 0, 1024, 2), (0, 96, 896, 128, 2))
N_PARTS = 4
BF16 = jnp.bfloat16
F32 = jnp.float32


def stage_dim(part, stage):
    return (PARTS[part][4] + stage) % 3


def last_stage(q, part):
    stage = -1
    for t in range(3):
        if q >> stage_dim(part, t) & 1:
            stage = t
    return stage


def log2(x):
    return jnp.log(x) * LOG2E


def nt(a, b):
    return lax.dot_general(a, b, (((1,), (1,)), ((), ())), preferred_element_type=F32)


def nn(a, b):
    return lax.dot_general(a, b, (((1,), (0,)), ((), ())), preferred_element_type=F32)


def tn(a, b):
    return lax.dot_general(a, b, (((0,), (0,)), ((), ())), preferred_element_type=F32)


def flip_image(c):
    return c + 1 - 2 * lax.rem(c, 2)


def flip_text(c):
    return 3 - c


def kernel(
    scale_ref, image_ref, text_ref,
    loss_out, image_out, text_out, scale_out,
    scale_s, feat_s, inv_s, lse_s, eye_s,
    img, txt, u_s, grad_s, flip_s, row_acc, col_acc, rows_s, cols_s,
    rowl_s, rowl_r, coll_s, coll_r, rlse_s, clse_s, crow_s,
    a_img, a_txt, core_s, core_r, rs_s, rs_r,
    part_s, part_r, part2_s, part2_r, part3_s, part3_r,
    load_sem, ag_send, ag_recv, core_send, core_recv,
    lse_send, lse_recv, csum_send, csum_recv, rs_send, rs_recv, tot_send, tot_recv,
):
    z = lax.axis_index("row")
    c = lax.axis_index("col")
    x, y, k = c // 8, lax.rem(c // 2, 4), lax.rem(c, 2)
    at = (x, y, z)
    flipped = (tuple(flip_image(v) for v in at), tuple(flip_text(v) for v in at))

    def place(side, q, other_core=0):
        px, py, pz = (flipped[side][d] if q >> d & 1 else at[d] for d in range(3))
        return {"row": pz, "col": (px * 4 + py) * 2 + (1 - k if other_core else k)}

    def remote(src, dst, send, recv, device):
        return pltpu.make_async_remote_copy(
            src_ref=src, dst_ref=dst, send_sem=send, recv_sem=recv, device_id=device, device_id_type=MESH
        )

    loads = [
        pltpu.make_async_copy(image_ref, feat_s.at[0], load_sem.at[0]),
        pltpu.make_async_copy(text_ref, feat_s.at[1], load_sem.at[1]),
        pltpu.make_async_copy(scale_ref, scale_s, load_sem.at[2]),
    ]
    for load in loads:
        load.start()
    def taken(ref, sem):
        pltpu.make_async_copy(ref, ref, sem).wait()

    peers = [place(0, 0, 1)] + [place(side, 1 << d) for side in range(2) for d in range(3)]
    barrier = pltpu.get_barrier_semaphore()
    for peer in peers:
        pl.semaphore_signal(barrier, inc=1, device_id=peer, device_id_type=MESH)

    def normalized(side):
        v = feat_s[side]
        return v * lax.rsqrt(jnp.sum(v * v, axis=1, keepdims=True) + EPS)

    loads[0].wait()
    img[pl.ds(0, CHUNK), :] = normalized(0).astype(BF16)
    loads[1].wait()
    txt[pl.ds(0, CHUNK), :] = normalized(1).astype(BF16)
    pl.semaphore_wait(barrier, len(peers))

    def area(part, base):
        row, rows, col, cols, _ = PARTS[part]
        return pl.ds(base + row, rows), pl.ds(col, cols)

    def gather_rows(side, q, part):
        return (img, txt)[side].at[area(part, RANK[q] * (2 * CHUNK if side == 0 else CHUNK))]

    def gather_copy(side, q, part):
        d = stage_dim(part, last_stage(q, part))
        i = (q - 1) * N_PARTS + part
        return remote(
            gather_rows(side, q ^ (1 << d), part), gather_rows(side, q, part),
            ag_send.at[side], ag_recv.at[side, i], place(side, 1 << d),
        )

    def core_copy(q, part):
        base = RANK[q] * 2 * CHUNK
        return remote(
            img.at[area(part, base)], img.at[area(part, base + CHUNK)],
            core_send.at[0], core_recv.at[q], place(0, 0, 1),
        )

    def arrive(q, first, *dims):
        for part in range(N_PARTS):
            if PARTS[part][4] == first:
                for side in range(2):
                    gather_copy(side, q, part).wait_recv()
                    for d in dims:
                        gather_copy(side, q | 1 << d, part).start()
                    if side == 0:
                        core_copy(q, part).start()

    def send_on(q, first):
        for part in range(N_PARTS):
            if PARTS[part][4] == first:
                for side in range(2):
                    gather_copy(side, q, part).start()

    def both_cores(*slots):
        for q in slots:
            taken(img.at[pl.ds(RANK[q] * 256 + CHUNK, CHUNK)], core_recv.at[q])


    for t in range(3):
        for d in range(3):
            send_on(1 << d, (d - t) % 3)
    for part in range(N_PARTS):
        core_copy(0, part).start()

    loads[2].wait()
    scale = jnp.exp(jnp.full((8, 128), scale_s[0], F32))[0:1, 0:1]
    unit = scale * LOG2E
    row_acc[...] = jnp.zeros_like(row_acc)
    col_acc[...] = jnp.zeros_like(col_acc)

    eye = lax.broadcasted_iota(jnp.int32, (CHUNK, CHUNK), 0) == lax.broadcasted_iota(jnp.int32, (CHUNK, CHUNK), 1)
    eye_s[pl.ds(0, CHUNK), :] = jnp.zeros((CHUNK, CHUNK), F32)
    eye_s[pl.ds(CHUNK, CHUNK), :] = jnp.where(eye, 1.0, 0.0)
    for side in range(2):
        v = feat_s[side]
        inverse = lax.rsqrt(jnp.sum(v * v, axis=1, keepdims=True) + EPS)
        feat_s[side] = v * inverse
        inv_s[side] = jnp.broadcast_to(inverse, (CHUNK, 128))

    def scores(row0, rows, col0, cols):
        for r in range(row0, row0 + rows, 256):
            u = nt(img[pl.ds(r, 256), :], txt[pl.ds(col0, cols), :]) * unit
            u_s[pl.ds(r, 256), pl.ds(col0, cols)] = u
            hi = jnp.exp2(u - SHIFT)
            lo = jnp.exp2(jnp.minimum(u, 0.0) + SHIFT)
            for i, e in enumerate((hi, lo, hi * u, lo * u)):
                row = e[:, 0:128]
                for j in range(1, cols // 128):
                    row = row + e[:, j * 128 : (j + 1) * 128]
                row_acc[i, pl.ds(r, 256), :] += row
                col_acc[i, :, pl.ds(col0, cols)] += jnp.sum(e.reshape(32, 8, cols), axis=0)

    def joined(hi, lo):
        return jnp.where(hi > TINY, log2(hi) + SHIFT, log2(lo) - SHIFT)

    def averaged(hi, lo, weighted_hi, weighted_lo):
        return jnp.where(hi > TINY, weighted_hi / hi, weighted_lo / lo)

    def absolute(side, q):
        bits = [lax.rem(v, 2) for v in at] if side == 0 else [v // 2 for v in at]
        bits = [1 - b if q >> d & 1 else b for d, b in enumerate(bits)]
        return bits[0] + 2 * bits[1] + 4 * bits[2]

    def row_index(q, other):
        return absolute(0, q) * 2 + (1 - k if other else k)

    def row_sums(q, kinds):
        for other in range(2):
            for i in kinds:
                row = row_acc[i, pl.ds(RANK[q] * 256 + other * CHUNK, CHUNK), :]
                rows_s[i, pl.ds(row_index(q, other), 1), :] = jnp.sum(row.T, axis=0, keepdims=True)

    def col_sums(kinds):
        for i in kinds:
            row = jnp.sum(col_acc[i], axis=0, keepdims=True)
            for q in range(8):
                cols_s[i, pl.ds(absolute(1, q), 1), :] = row[:, RANK[q] * 128 : (RANK[q] + 1) * 128]

    arrive(1, 0, 1, 2)
    arrive(4, 2, 0)
    arrive(2, 1, 2)
    arrive(1, 2, 1)
    arrive(2, 0, 2)
    arrive(4, 1, 0)
    send_on(3, 1)
    send_on(6, 2)
    arrive(1, 1)
    arrive(2, 2)
    arrive(4, 0)
    both_cores(0, 1, 2, 4)
    scores(0, 1024, 0, 512)
    arrive(5, 2, 1)
    arrive(3, 0, 2)
    arrive(5, 0)
    arrive(6, 1, 0)
    arrive(5, 1)
    both_cores(5)
    scores(1024, 256, 0, 512)
    scores(0, 1280, 512, 128)
    arrive(3, 2)
    arrive(3, 1)
    arrive(6, 2)
    arrive(6, 0)
    both_cores(3, 6)
    scores(1280, 512, 0, 512)
    scores(1280, 512, 512, 128)
    scores(0, 1792, 640, 256)
    for part in range(3):
        arrive(7, part)

    def gathered():
        taken(img.at[pl.ds(0, 7 * CHUNK)], ag_send.at[0])
        taken(txt.at[pl.ds(0, 7 * CHUNK)], ag_send.at[1])
        taken(img.at[pl.ds(0, 8 * CHUNK)], core_send.at[0])
        taken(rowl_r, lse_send.at[0])
        taken(coll_r, csum_send.at[0])

    scores(0, 1792, 896, 128)
    both_cores(7)
    scores(1792, 256, 0, 512)
    for q in ORDER[:7]:
        row_sums(q, (0, 1))
    scores(1792, 256, 512, 512)

    def matching(q, other):
        ix, iy, iz = (flipped[0][d] if q >> d & 1 else at[d] for d in range(3))
        ik = 1 - k if other else k
        tx, ty, tk, tz = iz, ix, iy // 2, lax.rem(iy, 2) * 2 + ik
        here = tk == k
        slot = 0
        for d, t in enumerate((tx, ty, tz)):
            across = t == flipped[1][d]
            here = here & (across | (t == at[d]))
            slot = slot + jnp.where(across, 1 << d, 0)
        rank = sum(jnp.where(slot == q, RANK[q], 0) for q in range(1, 8))
        return jnp.where(here, rank, -1)


    def row_copy(j):
        return remote(rowl_s, rowl_r.at[j - 1], lse_send.at[0], lse_recv.at[0], place(0, j >> 1, j & 1))

    def col_copy(q):
        return remote(coll_s, coll_r.at[q - 1], csum_send.at[0], csum_recv.at[0], place(1, q))

    col_sums((0, 1))
    coll_s[...] = joined(cols_s[0], cols_s[1])
    for q in (7, 3, 5, 6, 1, 2, 4):
        col_copy(q).start()
    row_sums(7, (0, 1))
    rowl_s[...] = joined(rows_s[0], rows_s[1])
    for j in (15, 14, 13, 12, 11, 10, 7, 6, 9, 8, 5, 4, 3, 2, 1):
        row_copy(j).start()
    part_s[...] = jnp.zeros_like(part_s)
    col_sums((2, 3))
    for q in range(8):
        row_sums(q, (2, 3))
    matches = [matching(q, other) for q in ORDER for other in range(2)]
    for i, rank in enumerate(matches):

        @pl.when(rank >= 0)
        def _():
            u = u_s[pl.ds(i * CHUNK, CHUNK), pl.ds(pl.multiple_of(rank * 128, 128), 128)]
            own = u * eye_s[pl.ds(CHUNK, CHUNK), :]
            own = jnp.sum(own.reshape(16, 8, 128), axis=0)
            part_s[pl.ds(0, 8), :] += -2.0 * own
            part_s[pl.ds(8, 8), :] += -own

    taken(coll_r, csum_recv.at[0])
    taken(rowl_r, lse_recv.at[0])

    def over(values):
        top = functools.reduce(jnp.maximum, values)
        return top + log2(functools.reduce(jnp.add, [jnp.exp2(v - top) for v in values]))

    rlse_s[...] = over([rowl_s[...]] + [rowl_r[j] for j in range(15)])
    clse_s[...] = over([coll_s[...]] + [coll_r[j] for j in range(7)])
    for q in range(8):
        crow_s[:, pl.ds(RANK[q] * 128, 128)] = clse_s[pl.ds(absolute(1, q), 1), :] + 1.0

    def spread(rank):
        for other in range(2):
            lse = rlse_s[pl.ds(row_index(ORDER[rank], other), 1), :] + 1.0
            lse_s[pl.ds(rank * 256 + other * CHUNK, CHUNK), :] = jnp.broadcast_to(lse, (CHUNK, CHUNK)).T

    def grads(blocks):
        for i, j in blocks:
            for other in range(2):
                here = pl.ds(i * 256 + other * CHUNK, CHUNK)
                at_col = pl.ds(j * 128, 128)
                u = u_s[here, at_col]
                flag = jnp.where(matches[i * 2 + other] == j, CHUNK, 0)
                own = eye_s[pl.ds(pl.multiple_of(flag, CHUNK), CHUNK), :]
                g = jnp.exp2(u - lse_s[here, :]) + jnp.exp2(u - crow_s[:, at_col]) - own
                low = g.astype(BF16)
                grad_s[here, at_col] = low
                flip_s[at_col, here] = low.T

    weighted = jnp.exp2(rowl_s[...] - rlse_s[...]) * averaged(*(rows_s[i] for i in range(4)))
    weighted = weighted[0:8] + weighted[8:16] + jnp.exp2(coll_s[...] - clse_s[...]) * averaged(*(cols_s[i] for i in range(4)))
    part_s[pl.ds(8, 8), :] += 0.5 * weighted
    part_s[pl.ds(0, 1), :] += rlse_s[pl.ds(row_index(0, 0), 1), :] + clse_s[pl.ds(absolute(1, 0), 1), :]

    def total_copy(stage, q):
        if stage == 0:
            return remote(part_s, part_r, tot_send.at[0], tot_recv.at[0], place(0, 0, 1))
        src, dst = ((part2_s, part2_r), (part3_s, part3_r))[stage - 1]
        return remote(src, dst.at[q - 1], tot_send.at[stage], tot_recv.at[stage], place(stage - 1, q))

    def row_blocks(rank):
        return [(rank, j) for j in range(rank + 1)]

    def col_blocks(rank):
        return [(i, rank) for i in range(rank)]

    def image_product(q):
        r = RANK[q] * 256
        for n in range(0, WIDTH, 256):
            acc = nn(grad_s[pl.ds(r, 256), :], txt[:, pl.ds(n, 256)])
            a_img[pl.ds(RANK[q] * CHUNK, CHUNK), pl.ds(n, 256)] = acc[0:CHUNK]
            core_s[pl.ds(q * CHUNK, CHUNK), pl.ds(n, 256)] = acc[CHUNK:].astype(BF16)

    def sibling(q):
        here = pl.ds(q * CHUNK, CHUNK)
        return remote(core_s.at[here], core_r.at[here], core_send.at[1], core_recv.at[8 + q], place(0, 0, 1))

    def text_product(q):
        here = pl.ds(RANK[q] * CHUNK, CHUNK)
        for n in range(0, WIDTH, 256):
            acc = nn(flip_s[here, :], img[:, pl.ds(n, 256)])
            a_txt[here, pl.ds(n, 256)] = acc
            if q:
                rs_s[1, pl.ds(q * CHUNK, CHUNK), pl.ds(n, 256)] = acc.astype(BF16)

    def region(q, part, stage):
        kept = [p for p in range(8) if all(not p >> stage_dim(part, t) & 1 for t in range(stage, 3))]
        return {2: 0, 1: 4, 0: 6}[stage] + kept.index(q)

    def sum_copy(side, q, part):
        stage = last_stage(q, part)
        d = stage_dim(part, stage)
        to = region(q ^ (1 << d), part, stage)
        i = to * N_PARTS + part
        return remote(
            rs_s.at[(side, *area(part, q * CHUNK))], rs_r.at[(side, *area(part, to * CHUNK))],
            rs_send.at[side], rs_recv.at[side, i], place(side, 1 << d),
        )

    def received(side, q, part, stage):
        sum_copy(side, q | 1 << stage_dim(part, stage), part).wait_recv()
        return rs_r[(side, *area(part, region(q, part, stage) * CHUNK))].astype(F32)

    def summed(side, q, part, upto):
        acc = (a_img, a_txt)[side][area(part, RANK[q] * CHUNK)]
        if side == 0:
            acc = acc + core_r[area(part, q * CHUNK)].astype(F32)
        for stage in range(2, upto, -1):
            acc = acc + received(side, q, part, stage)
        return acc

    def hand_on(side, q, part):
        if not (side == 1 and last_stage(q, part) == 2):
            rs_s[(side, *area(part, q * CHUNK))] = summed(side, q, part, last_stage(q, part)).astype(BF16)
        sum_copy(side, q, part).start()

    def rounds(side, slots, age):
        for q in slots:
            for part in range(N_PARTS):
                if 2 - last_stage(q, part) == age:
                    hand_on(side, q, part)

    def join(q):
        sibling(q).wait_recv()

    def step(done, q):
        image_product(q)
        text_product(done)
        rank = RANK[q]
        if rank:
            grads(col_blocks(rank) + row_blocks(rank - 1))
        sibling(q).start()
        rounds(1, (done,), 0)
        join(done)
        rounds(0, (done,), 0)

    def totals_1():
        taken(part_r, tot_recv.at[0])
        part2_s[...] = part_s[...] + part_r[...]
        for q in range(1, 8):
            total_copy(1, q).start()

    def totals_2():
        taken(part2_r, tot_recv.at[1])
        part3_s[...] = functools.reduce(jnp.add, [part2_s[...]] + [part2_r[j] for j in range(7)])
        for q in range(1, 8):
            total_copy(2, q).start()

    def corner(rank):
        grads(row_blocks(rank) + col_blocks(rank))

    def image_turn(q):
        image_product(q)
        sibling(q).start()

    def text_turn(q):
        text_product(q)
        rounds(1, (q,), 0)

    def join_turn(q):
        join(q)
        rounds(0, (q,), 0)

    total_copy(0, 0).start()
    for rank in range(7, -1, -1):
        spread(rank)
    corner(7)
    image_turn(7)
    text_turn(7)
    corner(6)
    image_turn(6)
    join_turn(7)
    text_turn(6)
    totals_1()
    corner(5)
    image_turn(3)
    join_turn(6)
    text_turn(3)
    corner(4)
    image_turn(5)
    join_turn(3)
    text_turn(5)
    totals_2()
    rounds(1, (6, 3, 5), 1)
    corner(3)
    image_turn(4)
    join_turn(5)
    rounds(0, (6, 3, 5), 1)
    text_turn(4)
    corner(2)
    image_turn(2)
    join_turn(4)
    text_turn(2)
    rounds(1, (4,), 1)
    corner(1)
    corner(0)
    image_turn(1)
    join_turn(2)
    rounds(0, (4,), 1)
    text_turn(1)
    rounds(1, (2, 1), 1)
    image_turn(0)
    join_turn(1)
    rounds(0, (2, 1), 1)
    text_product(0)
    rounds(1, (4, 2, 1), 2)
    rounds(0, (4, 2, 1), 2)
    join(0)

    outs = (image_out, text_out)
    for side in (1, 0):
        for part in range(N_PARTS):
            outs[side][area(part, 0)] = summed(side, 0, part, 0)
    for side in (1, 0):
        for part in range(N_PARTS):
            outs[side][area(part, 0)] += received(side, 0, part, 0)
        hat, g = feat_s[side], outs[side][...] * scale
        inverse = inv_s[side][:, 0:1]
        outs[side][...] = inverse * (g - hat * jnp.sum(hat * g, axis=1, keepdims=True))

    taken(part3_r, tot_recv.at[2])
    totals = functools.reduce(jnp.add, [part3_s[...]] + [part3_r[j] for j in range(7)])
    pairs = 128.0 * CHUNK
    loss_out[0] = jnp.sum(totals[0:8]) * (LN2 / (2.0 * pairs))
    scale_out[0] = jnp.sum(totals[8:16]) * (LN2 / pairs)

    taken(rs_r.at[0], rs_send.at[0])
    taken(rs_r.at[1], rs_send.at[1])
    taken(core_s, core_send.at[1])
    taken(part_r, tot_send.at[0])
    taken(part2_r, tot_send.at[1])
    taken(part3_r, tot_send.at[2])
    gathered()


def local(image_features, text_features, logit_scale):
    hbm = pl.BlockSpec(memory_space=pltpu.HBM)
    vmem = pl.BlockSpec(memory_space=pltpu.VMEM)
    smem = pl.BlockSpec(memory_space=pltpu.SMEM)
    dma = pltpu.SemaphoreType.DMA
    results = pl.pallas_call(
        kernel,
        out_shape=(
            pltpu.SMEM((1,), F32),
            pltpu.VMEM((CHUNK, WIDTH), F32),
            pltpu.VMEM((CHUNK, WIDTH), F32),
            pltpu.SMEM((1,), F32),
        ),
        in_specs=[hbm] * 3,
        out_specs=(smem, vmem, vmem, smem),
        scratch_shapes=[
            pltpu.SMEM((1,), F32),
            pltpu.VMEM((2, CHUNK, WIDTH), F32),
            pltpu.VMEM((2, CHUNK, 128), F32),
            pltpu.VMEM((2048, 128), F32),
            pltpu.VMEM((2 * CHUNK, CHUNK), F32),
            pltpu.VMEM((2048, WIDTH), BF16),
            pltpu.VMEM((1024, WIDTH), BF16),
            pltpu.VMEM((2048, 1024), F32),
            pltpu.VMEM((2048, 1024), BF16),
            pltpu.VMEM((1024, 2048), BF16),
            pltpu.VMEM((4, 2048, 128), F32),
            pltpu.VMEM((4, 8, 1024), F32),
            pltpu.VMEM((4, 16, 128), F32),
            pltpu.VMEM((4, 8, 128), F32),
            pltpu.VMEM((16, 128), F32),
            pltpu.VMEM((15, 16, 128), F32),
            pltpu.VMEM((8, 128), F32),
            pltpu.VMEM((7, 8, 128), F32),
            pltpu.VMEM((16, 128), F32),
            pltpu.VMEM((8, 128), F32),
            pltpu.VMEM((1, 1024), F32),
            pltpu.VMEM((1024, WIDTH), F32),
            pltpu.VMEM((1024, WIDTH), F32),
            pltpu.VMEM((1024, WIDTH), BF16),
            pltpu.VMEM((1024, WIDTH), BF16),
            pltpu.VMEM((2, 1024, WIDTH), BF16),
            pltpu.VMEM((2, 7 * CHUNK, WIDTH), BF16),
            pltpu.VMEM((16, 128), F32),
            pltpu.VMEM((16, 128), F32),
            pltpu.VMEM((16, 128), F32),
            pltpu.VMEM((7, 16, 128), F32),
            pltpu.VMEM((16, 128), F32),
            pltpu.VMEM((7, 16, 128), F32),
            dma((3,)),
            dma((2,)),
            dma((2, 7 * N_PARTS)),
            dma((2,)),
            dma((16,)),
            dma((1,)),
            dma((1,)),
            dma((1,)),
            dma((1,)),
            dma((2,)),
            dma((2, 7 * N_PARTS)),
            dma((3,)),
            dma((3,)),
        ],
        compiler_params=pltpu.CompilerParams(
            collective_id=0, has_side_effects=True, vmem_limit_bytes=60 * 2**20
        ),
        name="contrastive",
    )(logit_scale, image_features, text_features)
    return results


def solution(mesh):
    in_specs = (P(("row", "col"), None), P(("col", "row"), None), P())
    out_specs = (P(), P(("row", "col"), None), P(("col", "row"), None), P())
    return jax.shard_map(local, mesh=mesh, in_specs=in_specs, out_specs=out_specs, check_vma=False)
```
